128 devices in a mesh: energy: 16 (over z, y), slab: 8 (over x, core).
Axes of the slice: x: 4, y: 4, z: 4, core: 2. Of those that a mesh axis runs over, the one named last changes fastest.
Arguments:
- occupancy: int32 [16, 256], P('slab', 'energy'), may hold values from 0 to 2
- onsite: float32 [16, 256], P('slab', 'energy'), may hold values from 0 to 1
- defect_shift: float32 [16, 256], P('slab', 'energy'), may hold values from 0.3 to 1.5
- site_order: int32 [256], replicated, may hold values from 0 to 255, each once
- lateral: float32 [16, 256, 256], P('slab', 'energy'), may hold values from -4.5 to 4.5
- coupling: float32 [16, 256], P('slab'), may hold values from 2 to 3
- energies: float32 [16], P('energy'), may hold values from 1.5 to 3.5
- weights: float32 [16], P('energy'), may hold values from 0.05 to 0.25
- sources: float32 [2, 16, 16, 256], P(None, 'energy', 'slab'), may hold values from -6 to 6
Outputs:
- site_density: float32 [16, 256], P('slab', 'energy')
The draws below stay inside these ranges and needn't reach their ends.
Inputs may be any that keep to these rules, and one draw needn't show every extreme that they name: `site_order`: a permutation of the 256 orbitals of a block.
All inputs are finite; a program needn't handle non-finite values.
Results may differ from the reference program's by a relative error of at most 0.0003.
Values sent between devices are 32-bit elements; how exact they have to be, the bound alone decides.
No kernel may reach another device: no remote copies, remote signals or barrier semaphores. Data moves between devices by JAX's collectives and lax.ppermute only.
A program may use at most 128 MiB of HBM per device.

```python
import math
import jax
import jax.numpy as jnp
from jax import lax

B = 256
NB = 16
NE = 16


def place_ends(values, key, low, largest):
    longest = values.shape.index(max(values.shape))
    spots = []
    for shift in (0, 1):
        where = [jax.random.randint(jax.random.fold_in(key, axis), (), 0, length) for axis, length in enumerate(values.shape)]
        where[longest] = (where[longest] + shift) % values.shape[longest]
        spots.append(tuple(where))
    return values.at[spots[0]].set(low).at[spots[1]].set(largest)


def levels(key, shape, shards, smallest, high):
    gain, own = 1.0, jax.random.fold_in(key, 6)
    for position, parts in shards:
        steps = jnp.exp(jax.random.uniform(jax.random.fold_in(own, position), (parts,), jnp.float32, smallest / len(shards), high / len(shards)))
        gain = gain * jnp.repeat(steps, shape[position] // parts).reshape([-1 if axis == position else 1 for axis in range(len(shape))])
    return gain


def centred(own_key, dims, scale, limit, split=(), held_as=jnp.bfloat16):
    values = scale * jax.random.normal(own_key, dims, jnp.float32)
    if split:
        values = values * levels(own_key, dims, split, -0.22, 0.18)
    return jnp.clip(values, -limit, limit).astype(held_as)


def setup_inputs(seed: int = 0) -> dict:
    streams_of = jax.random.split(jax.random.key(seed), 10)
    return {
        "occupancy": place_ends(jax.random.randint(streams_of[0], (NB, B), 0, 3), jax.random.fold_in(streams_of[0], 1), 0, 2).astype(jnp.int32),
        "onsite": jnp.clip(1.0 * jax.random.uniform(streams_of[1], (NB, B), jnp.float32) ** levels(streams_of[1], (NB, B), ((0, 8), (1, 16)), -0.2, 0.2), 0.0, 1.0),
        "defect_shift": jnp.clip(jnp.exp(math.log(1.5) - 1.60943787 * jax.random.uniform(streams_of[2], (NB, B), jnp.float32) ** levels(streams_of[2], (NB, B), ((0, 8), (1, 16)), -0.2, 0.2)), 0.3, 1.5),
        "site_order": jax.random.permutation(streams_of[3], B).astype(jnp.int32),
        "lateral": centred(streams_of[4], (NB, B, B), 0.75, 4.5, ((0, 8), (1, 16)), jnp.float32),
        "coupling": jnp.clip(2.0 + 1.0 * jax.random.uniform(streams_of[5], (NB, B), jnp.float32) ** levels(streams_of[5], (NB, B), ((0, 8),), -0.2, 0.2), 2.0, 3.0),
        "energies": jnp.clip(1.5 + 2.0 * jax.random.uniform(streams_of[6], (NE,), jnp.float32) ** levels(streams_of[6], (NE,), ((0, 16),), -0.2, 0.2), 1.5, 3.5),
        "weights": jnp.clip(jnp.exp(math.log(0.25) - 1.609438 * jax.random.uniform(streams_of[7], (NE,), jnp.float32) ** levels(streams_of[7], (NE,), ((0, 16),), -0.2, 0.2)), 0.05, 0.25),
        "sources": centred(streams_of[8], (2, NE, NB, B), 1.0, 6.0, ((1, 16), (2, 8)), jnp.float32),
    }


BROADENING = 1.2
LATERAL_SCALE = 0.9

def solve_complex(matrix_re, matrix_im, target_re, target_im):
    upper_half = jnp.concatenate([matrix_re, -matrix_im], axis=1)
    lower_half = jnp.concatenate([matrix_im, matrix_re], axis=1)
    system = jnp.concatenate([upper_half, lower_half], axis=0)
    answer = jnp.linalg.solve(system, jnp.concatenate([target_re, target_im], axis=0))
    width = matrix_re.shape[0]
    return (answer[:width], answer[width:])

def mat_vector(matrix, vector):
    return jnp.dot(matrix.astype(jnp.float32), vector.astype(jnp.float32), precision=lax.Precision.HIGHEST, preferred_element_type=jnp.float32)

def reference(occupancy, onsite, defect_shift, site_order, lateral, coupling, energies, weights, sources):
    brick_pot = onsite + occupancy.astype(jnp.float32) * defect_shift
    potential = jnp.zeros_like(brick_pot).at[:, site_order].set(brick_pot)
    hopping = LATERAL_SCALE * (lateral + jnp.swapaxes(lateral, 1, 2))
    width = coupling.shape[1]
    identity = jnp.eye(width, dtype=jnp.float32)
    bond_before = jnp.concatenate([jnp.zeros_like(coupling[:1]), coupling[:-1]], axis=0)
    bond_after = jnp.concatenate([coupling[:-1], jnp.zeros_like(coupling[:1])], axis=0)

    def one_energy(density, inputs):
        energy, weight, source = inputs

        def forward(state, items):
            prev_z_re, prev_z_im, prev_q_re, prev_q_im = state
            pot_row, hop_block, before, after, src_re, src_im = items
            schur_re = (energy - pot_row)[:, None] * identity - hop_block - before[:, None] * prev_z_re
            schur_im = BROADENING * identity - before[:, None] * prev_z_im
            right_re = src_re + before * prev_q_re
            right_im = src_im + before * prev_q_im
            target_re = jnp.concatenate([after[:, None] * identity, right_re[:, None]], axis=1)
            target_im = jnp.concatenate([jnp.zeros_like(identity), right_im[:, None]], axis=1)
            out_re, out_im = solve_complex(schur_re, schur_im, target_re, target_im)
            new_state = (out_re[:, :width], out_im[:, :width], out_re[:, width], out_im[:, width])
            return (new_state, new_state)
        zero_mat = jnp.zeros((width, width), jnp.float32)
        zero_vec = jnp.zeros((width,), jnp.float32)
        initial = (zero_mat, zero_mat, zero_vec, zero_vec)
        _, stacked = lax.scan(forward, initial, (potential, hopping, bond_before, bond_after, source[0], source[1]))

        def backward(state, items):
            next_re, next_im = state
            z_re, z_im, q_re, q_im = items
            psi_re = q_re + mat_vector(z_re, next_re) - mat_vector(z_im, next_im)
            psi_im = q_im + mat_vector(z_re, next_im) + mat_vector(z_im, next_re)
            return ((psi_re, psi_im), (psi_re, psi_im))
        _, (all_re, all_im) = lax.scan(backward, (zero_vec, zero_vec), stacked, reverse=True)
        density = density + weight * (all_re * all_re + all_im * all_im)
        return (density, None)
    density, _ = lax.scan(one_energy, jnp.zeros_like(brick_pot), (energies, weights, jnp.moveaxis(sources, 1, 0)))
    return density
```

```python
import functools
import jax
import jax.numpy as jnp
from jax import lax
from jax.experimental import pallas as pl
from jax.experimental.pallas import tpu as pltpu
from jax.sharding import PartitionSpec as P

BROADENING = 1.2
LATERAL_SCALE = 0.9
HIGHEST = lax.Precision.HIGHEST
PACK = 2 * 256 + 8
N=256
W=32
S8=(8,128)
def row(t,s): return jnp.broadcast_to(t[s:s+1],S8)
def lane_of(t,idx): return jnp.take_along_axis(t,idx,axis=1)
def split3(x):
    h=x.astype(jnp.bfloat16); r=x-h.astype(jnp.float32)
    m=r.astype(jnp.bfloat16); l=(r-m.astype(jnp.float32)).astype(jnp.bfloat16)
    return h,m,l
def panel(T,place,sub,lane):
    half=place//128; off=place-128*half
    nt=W//8
    Z=[]
    for s in range(nt):
        pick=lambda t: tuple(jnp.where(half==0,T[t][0][c],T[t][1][c]) for c in (0,1))
        idx=[jnp.full(S8,off+8*s+j,jnp.int32) for j in range(8)]
        src=pick(s)
        C=[(lane_of(src[0],idx[j]),lane_of(src[1],idx[j])) for j in range(8)]
        O={}
        for t in range(s+1,nt):
            o=pick(t)
            O[t]=[(lane_of(o[0],idx[j]),lane_of(o[1],idx[j])) for j in range(8)]
        first=place+8*s
        for h in range(2):
            local=lane-(first-128*h)
            inside=(local>=0)&(local<8)
            minus=jnp.where(local==sub,-1.0,0.0)
            for t in range(s,nt):
                r,i=T[t][h]
                T[t][h]=(jnp.where(inside,minus if t==s else 0.0,r),jnp.where(inside,0.0,i))
        X=[T[s][0],T[s][1]]
        Qr=Qi=None
        rows=[[],[]]
        for j in range(8):
            cr,ci=C[j]
            pr=row(cr,j); pi=row(ci,j)
            inv=1.0/(pr*pr+pi*pi)
            qr=pr*inv; qi=-pi*inv
            Qr=qr if j==0 else jnp.where(sub==j,qr,Qr)
            Qi=qi if j==0 else jnp.where(sub==j,qi,Qi)
            if j<7:
                below=sub>j
                cr=jnp.where(below,cr,0.0); ci=jnp.where(below,ci,0.0)
            def scaled(x,fast=False):
                r=row(x[0],j); i=row(x[1],j)
                if fast: return (r*pr+i*pi)*inv,(i*pr-r*pi)*inv
                return r*qr-i*qi,i*qr+r*qi
            def step(x,w):
                return (x[0]-(cr*w[0]-ci*w[1]),x[1]-(cr*w[1]+ci*w[0]))
            for j2 in range(j+1,8):
                w=scaled(C[j2],j2==j+1)
                C[j2]=step(C[j2],w)
                for t in range(s+1,nt):
                    o,o2=O[t][j],O[t][j2]
                    O[t][j2]=(o2[0]-(o[0]*w[0]-o[1]*w[1]),o2[1]-(o[0]*w[1]+o[1]*w[0]))
            for h in range(2):
                w=scaled(X[h])
                rows[h].append(w)
                if j<7: X[h]=step(X[h],w)
        T[s]=X
        Z.append([(x[0]*Qr-x[1]*Qi,x[1]*Qr+x[0]*Qi) for x in X])
        for t in range(s+1,nt):
            for h in range(2):
                r,i=T[t][h]
                for j in range(8):
                    cr,ci=O[t][j]; vr,vi=rows[h][j]
                    r=r-(cr*vr-ci*vi); i=i-(cr*vi+ci*vr)
                T[t][h]=(r,i)
    for t in range(nt-1):
        for h in range(2):
            local=lane-(place-128*h)
            above=(local>=8*t+8)&(local<W)
            T[t][h]=tuple(jnp.where(above,0.0,x) for x in T[t][h])
            Z[t][h]=tuple(jnp.where(above,0.0,x) for x in Z[t][h])
    return T,Z
PR=((0,0),(0,1),(1,0),(1,1),(0,2),(2,0))
def invert(ar,ai):
    sub=lax.broadcasted_iota(jnp.int32,S8,0); lane=lax.broadcasted_iota(jnp.int32,S8,1)
    @pl.loop(0,N//W)
    def _(k):
        place=pl.multiple_of(k*W,W)
        old=[ar[pl.ds(place,W),:],ai[pl.ds(place,W),:]]
        T=[[tuple(old[c][8*t:8*t+8,128*h:128*h+128] for c in (0,1)) for h in (0,1)] for t in range(W//8)]
        Y,Z=panel(T,place,sub,lane)
        whole=lambda M: [jnp.concatenate([jnp.concatenate([m[0][c],m[1][c]],1) for m in M],0) for c in (0,1)]
        ys=[split3(u) for u in whole(Y)]; zs=[split3(v) for v in whole(Z)]; ns=[-v for v in zs[1]]
        left=jnp.concatenate([ys[0][a] for a,_ in PR]+[ys[1][a] for a,_ in PR],0)
        re=jnp.concatenate([zs[0][b] for _,b in PR]+[ns[b] for _,b in PR],0)
        im=jnp.concatenate([zs[1][b] for _,b in PR]+[zs[0][b] for _,b in PR],0)
        right=jnp.concatenate([re,im],1)
        out=lax.dot_general(left,right,(((0,),(0,)),((),())),preferred_element_type=jnp.float32)
        full=lax.broadcasted_iota(jnp.int32,(1,N),1)-place
        keep=jnp.broadcast_to((full<0)|(full>=W),(N,N))
        ar[pl.ds(place,W),:]=jnp.zeros((W,N),jnp.float32)
        ai[pl.ds(place,W),:]=jnp.zeros((W,N),jnp.float32)
        ar[...]=jnp.where(keep,ar[...],0.0)-out[:,:N]
        ai[...]=jnp.where(keep,ai[...],0.0)-out[:,N:]


def prep_kernel(flag, got, vecs, out):
    turned = flag[0]
    for b in range(2):
        rows = jnp.concatenate([got[e, 16 * b : 16 * b + 16, :] for e in range(16)], 0)
        hop = LATERAL_SCALE * (rows + rows.T)
        pot = got[0, 32 + b : 33 + b, :]
        for e in range(1, 16):
            pot = pot + got[e, 32 + b : 33 + b, :]
        on_diag = lax.broadcasted_iota(jnp.int32, (N, N), 0) == lax.broadcasted_iota(
            jnp.int32, (N, N), 1
        )
        place = jnp.where(turned == 1, 1 - b, b) * N
        out[pl.ds(pl.multiple_of(place, N), N), :] = jnp.where(on_diag, -pot - hop, -hop)
    out[2 * N : 2 * N + 8, :] = vecs[...]


def row_times(vector, matrix):
    return jnp.dot(vector, matrix, precision=HIGHEST, preferred_element_type=jnp.float32)


def apply(vr, vi, gr, gi):
    both = jnp.concatenate([vr, vi, jnp.zeros((6, N), jnp.float32)], 0)
    a = row_times(both, gr)
    b = row_times(both, gi)
    return b[1:2] - a[0:1], -a[1:2] - b[0:1]


def load_block(ar, ai, real, link, energy):
    across = jnp.broadcast_to(link, (N, N))
    scale = across * across.T
    on_diag = lax.broadcasted_iota(jnp.int32, (N, N), 0) == lax.broadcasted_iota(
        jnp.int32, (N, N), 1
    )
    ar[...] = real + scale * ar[...] + jnp.where(on_diag, energy, 0.0)
    ai[...] = scale * ai[...] + jnp.where(on_diag, BROADENING, 0.0)


def chain_kernel(flag, energy, pack, start, before, mats, vecs, ar, ai, carry):
    ar[...] = start[1, 0]
    ai[...] = start[1, 1]
    carry[...] = before[1]

    @pl.loop(0, 2)
    def _(b):
        here = pack[2 * N : 2 * N + 8, :]
        pick = lambda i: jnp.where(b == 0, here[i : i + 1], here[i + 1 : i + 2])
        bond, src_r, src_i = pick(0), pick(2), pick(4)
        link = jnp.where(flag[0] == 1, bond, carry[3:4, :])
        load_block(ar, ai, pack[pl.ds(pl.multiple_of(b * N, N), N), :], link, energy[0])
        rhs_r = src_r + link * carry[0:1, :]
        rhs_i = src_i + link * carry[1:2, :]
        invert(ar, ai)
        mats[b, 0] = ar[...]
        mats[b, 1] = ai[...]
        q_r, q_i = apply(rhs_r, rhs_i, ar[...], ai[...])
        now = jnp.concatenate(
            [q_r, q_i, link, bond, rhs_r, rhs_i, jnp.zeros((2, N), jnp.float32)], 0
        )
        carry[...] = now
        vecs[b] = now


def last_kernel(
    flag, energy, weight, pack, m0, m1, m2, m3, v0, v1, v2, v3, far_m, far_v, out, ar, ai
):
    all_m = [m0, m1, m2, m3]
    all_v = [v0, v1, v2, v3]
    middle = jnp.where(flag[0] == 1, far_v[3:4, :], v3[1, 3:4, :])
    ar[...] = m3[0, 0]
    ai[...] = m3[0, 1]
    load_block(ar, ai, pack[N : 2 * N, :], v3[1, 2:3, :], energy[0])
    across = jnp.broadcast_to(middle, (N, N))
    scale = across * across.T
    ar[...] = ar[...] + scale * far_m[0]
    ai[...] = ai[...] + scale * far_m[1]
    rhs_r = v3[1, 4:5, :] + middle * far_v[0:1, :]
    rhs_i = v3[1, 5:6, :] + middle * far_v[1:2, :]
    invert(ar, ai)
    now_r, now_i = apply(rhs_r, rhs_i, ar[...], ai[...])
    rows = [weight[0] * (now_r * now_r + now_i * now_i)]
    for j in range(6, -1, -1):
        link = all_v[(j + 1) // 2][(j + 1) % 2, 2:3, :]
        vec = all_v[j // 2]
        b = j % 2
        add_r, add_i = apply(link * now_r, link * now_i, all_m[j // 2][b, 0], all_m[j // 2][b, 1])
        now_r = vec[b, 0:1, :] + add_r
        now_i = vec[b, 1:2, :] + add_i
        rows.append(weight[0] * (now_r * now_r + now_i * now_i))
    out[...] = jnp.concatenate(rows[::-1], 0)


SMEM = pl.BlockSpec(memory_space=pltpu.SMEM)
VMEM = pl.BlockSpec(memory_space=pltpu.VMEM)
PARAMS = pltpu.CompilerParams(vmem_limit_bytes=48 * 2**20)
MATRIX = pltpu.VMEM((N, N), jnp.float32)


def shape(*dims):
    return jax.ShapeDtypeStruct(dims, jnp.float32)


def prep(flag, got, vecs):
    return pl.pallas_call(
        prep_kernel,
        out_shape=shape(PACK, N),
        in_specs=[SMEM, VMEM, VMEM],
        out_specs=VMEM,
        compiler_params=PARAMS,
    )(flag, got, vecs)


def chain(flag, energy, pack, start, before):
    return pl.pallas_call(
        chain_kernel,
        out_shape=[shape(2, 2, N, N), shape(2, 8, N)],
        in_specs=[SMEM, SMEM, VMEM, VMEM, VMEM],
        out_specs=[VMEM, VMEM],
        scratch_shapes=[MATRIX, MATRIX, pltpu.VMEM((8, N), jnp.float32)],
        compiler_params=PARAMS,
    )(flag, energy, pack, start, before)


def last(flag, energy, weight, pack, mats, vecs, far_m, far_v):
    return pl.pallas_call(
        last_kernel,
        out_shape=shape(8, N),
        in_specs=[SMEM] * 3 + [VMEM] * 11,
        out_specs=VMEM,
        scratch_shapes=[MATRIX, MATRIX],
        compiler_params=PARAMS,
    )(flag, energy, weight, pack, *mats, *vecs, far_m, far_v)


def shards(
    occupancy, onsite, defect_shift, site_order, lateral, coupling, energies, weights, sources
):
    slab = lax.axis_index("slab")
    column = lax.axis_index("energy")
    pot_piece = onsite + occupancy.astype(jnp.float32) * defect_shift
    mine = lax.dynamic_slice(site_order, (column * 16,), (16,))
    at = mine[:, None] == lax.broadcasted_iota(jnp.int32, (16, N), 1)
    spread = jnp.sum(jnp.where(at[None], pot_piece[:, :, None], 0.0), axis=1)
    piece = jnp.concatenate([lateral.reshape(32, N), spread, jnp.zeros((6, N), jnp.float32)], 0)
    got = lax.all_to_all(jnp.broadcast_to(piece[None], (16, 40, N)), "energy", 0, 0)
    flip = slab >= 4
    flag = flip.astype(jnp.int32)[None]
    vecs = jnp.stack([coupling, sources[0, 0], sources[1, 0]])
    vecs = jnp.where(flip, vecs[:, ::-1], vecs).reshape(6, N)
    vecs = jnp.concatenate([vecs, jnp.zeros((2, N), jnp.float32)], 0)
    own = prep(flag, got, vecs)
    packs = [
        own,
        lax.ppermute(own, "slab", [(1, 0), (6, 7)]),
        lax.ppermute(own, "slab", [(2, 0), (5, 7)]),
        lax.ppermute(own, "slab", [(3, 0), (4, 7)]),
    ]
    start = jnp.zeros((2, 2, N, N), jnp.float32)
    before = jnp.zeros((2, 8, N), jnp.float32)
    mats, vecs = [], []
    for pack in packs:
        start, before = chain(flag, energies, pack, start, before)
        mats.append(start)
        vecs.append(before)
    swap = [(0, 7), (7, 0)]
    far_m, far_v = lax.ppermute((start[1], before[1]), "slab", swap)
    density = last(flag, energies, weights, packs[3], mats, vecs, far_m, far_v)
    density = jnp.where(flip, density[::-1], density)
    parts = density.reshape(4, 2, 16, 16)
    low = jnp.where(slab == 0, parts, 0.0)
    high = jnp.where(slab == 7, parts, 0.0)
    sent = jnp.concatenate([low, high], 0).transpose(0, 2, 1, 3).reshape(128, 2, 16)
    return jnp.sum(lax.all_to_all(sent, ("slab", "energy"), 0, 0), axis=0)


def solution(mesh):
    return jax.shard_map(
        shards,
        mesh=mesh,
        in_specs=(
            P("slab", "energy"),
            P("slab", "energy"),
            P("slab", "energy"),
            P(),
            P("slab", "energy", None),
            P("slab", None),
            P("energy"),
            P("energy"),
            P(None, "energy", "slab", None),
        ),
        out_specs=P("slab", "energy"),
        check_vma=False,
    )
```

```python
import functools
import jax
import jax.numpy as jnp
from jax import lax
from jax.experimental import pallas as pl
from jax.experimental.pallas import tpu as pltpu
from jax.sharding import PartitionSpec as P

BROADENING = 1.2
LATERAL_SCALE = 0.9
HIGHEST = lax.Precision.HIGHEST
PACK = 2 * 256 + 8
N=256
W=32
S8=(8,128)
def row(t,s): return jnp.broadcast_to(t[s:s+1],S8)
def lane_of(t,idx): return jnp.take_along_axis(t,idx,axis=1)
def split3(x):
    h=x.astype(jnp.bfloat16); r=x-h.astype(jnp.float32)
    m=r.astype(jnp.bfloat16); l=(r-m.astype(jnp.float32)).astype(jnp.bfloat16)
    return h,m,l
MIX=True
def times(x,y): return (x[0]*y[0]-x[1]*y[1],x[0]*y[1]+x[1]*y[0])
def less(x,a,b): return (x[0]-(a[0]*b[0]-a[1]*b[1]),x[1]-(a[0]*b[1]+a[1]*b[0]))
def row2(x,j): return (row(x[0],j),row(x[1],j))
def panel(T,place,sub,lane):
    half=place//128; off=place-128*half
    nt=W//8
    Z=[]
    for s in range(nt):
        pick=lambda t: tuple(jnp.where(half==0,T[t][0][c],T[t][1][c]) for c in (0,1))
        idx=[jnp.full(S8,off+8*s+j,jnp.int32) for j in range(8)]
        wide=lambda x: [tuple(lane_of(c,idx[j]) for c in x) for j in range(8)]
        C=wide(pick(s))
        O={t:wide(pick(t)) for t in range(s+1,nt)}
        first=place+8*s
        for h in range(2):
            local=lane-(first-128*h)
            inside=(local>=0)&(local<8)
            minus=jnp.where(local==sub,-1.0,0.0)
            for t in range(s,nt):
                r,i=T[t][h]
                T[t][h]=(jnp.where(inside,minus if t==s else 0.0,r),jnp.where(inside,0.0,i))
        X=[T[s][0],T[s][1]]
        Q=None
        rows=[[],[]]
        p=row2(C[0],0)
        for j in range(8):
            inv=1.0/(p[0]*p[0]+p[1]*p[1])
            c=C[j]
            q=(p[0]*inv,-p[1]*inv)
            Q=q if j==0 else tuple(jnp.where(sub==j,a,b) for a,b in zip(q,Q))
            if j<7:
                e=row2(c,j+1)
                g=times(times(e,e),(p[0],-p[1]))
                n=row2(C[j+1],j+1)
                p=(n[0]-g[0]*inv,n[1]-g[1]*inv)
                low=tuple(jnp.where(sub>j,a,0.0) for a in c)
                scaled=times(c,q)
                for j2 in range(j+1,8):
                    w=row2(scaled,j2)
                    C[j2]=less(C[j2],low,w)
                    for t in range(s+1,min(nt,s+2) if MIX else nt): O[t][j2]=less(O[t][j2],O[t][j],w)
            for h in range(2):
                w=times(row2(X[h],j),q)
                rows[h].append(w)
                if j<7: X[h]=less(X[h],low,w)
        T[s]=X
        z=[times(x,Q) for x in X]
        Z.append(z)
        if s<nt-1:
            for h in range(2):
                x=T[s+1][h]
                for j in range(8): x=less(x,O[s+1][j],rows[h][j])
                T[s+1][h]=x
        if s<nt-2:
            if MIX:
                V=list(z)
                for j in range(7,0,-1):
                    u=times(C[j],Q)
                    u=tuple(jnp.where(sub<j,a,0.0) for a in u)
                    V=[less(v,u,row2(v,j)) for v in V]
                rows=[[row2(v,j) for j in range(8)] for v in V]
            for t in range(s+2,nt):
                for h in range(2):
                    x=T[t][h]
                    for j in range(8): x=less(x,O[t][j],rows[h][j])
                    T[t][h]=x
    for t in range(nt-1):
        for h in range(2):
            local=lane-(place-128*h)
            above=(local>=8*t+8)&(local<W)
            T[t][h]=tuple(jnp.where(above,0.0,x) for x in T[t][h])
            Z[t][h]=tuple(jnp.where(above,0.0,x) for x in Z[t][h])
    return T,Z
PR=((0,0),(0,1),(1,0),(1,1),(0,2),(2,0))
def invert(ar,ai):
    sub=lax.broadcasted_iota(jnp.int32,S8,0); lane=lax.broadcasted_iota(jnp.int32,S8,1)
    @pl.loop(0,N//W)
    def _(k):
        place=pl.multiple_of(k*W,W)
        old=[ar[pl.ds(place,W),:],ai[pl.ds(place,W),:]]
        T=[[tuple(old[c][8*t:8*t+8,128*h:128*h+128] for c in (0,1)) for h in (0,1)] for t in range(W//8)]
        Y,Z=panel(T,place,sub,lane)
        whole=lambda M: [jnp.concatenate([jnp.concatenate([m[0][c],m[1][c]],1) for m in M],0) for c in (0,1)]
        ys=[split3(u) for u in whole(Y)]; zs=[split3(v) for v in whole(Z)]; ns=[-v for v in zs[1]]
        left=jnp.concatenate([ys[0][a] for a,_ in PR]+[ys[1][a] for a,_ in PR],0)
        re=jnp.concatenate([zs[0][b] for _,b in PR]+[ns[b] for _,b in PR],0)
        im=jnp.concatenate([zs[1][b] for _,b in PR]+[zs[0][b] for _,b in PR],0)
        right=jnp.concatenate([re,im],1)
        out=lax.dot_general(left,right,(((0,),(0,)),((),())),preferred_element_type=jnp.float32)
        full=lax.broadcasted_iota(jnp.int32,(1,N),1)-place
        keep=jnp.broadcast_to((full<0)|(full>=W),(N,N))
        ar[pl.ds(place,W),:]=jnp.zeros((W,N),jnp.float32)
        ai[pl.ds(place,W),:]=jnp.zeros((W,N),jnp.float32)
        ar[...]=jnp.where(keep,ar[...],0.0)-out[:,:N]
        ai[...]=jnp.where(keep,ai[...],0.0)-out[:,N:]


def prep_kernel(flag, got, vecs, out):
    turned = flag[0]
    for b in range(2):
        rows = jnp.concatenate([got[e, 16 * b : 16 * b + 16, :] for e in range(16)], 0)
        hop = LATERAL_SCALE * (rows + rows.T)
        pot = got[0, 32 + b : 33 + b, :]
        for e in range(1, 16):
            pot = pot + got[e, 32 + b : 33 + b, :]
        on_diag = lax.broadcasted_iota(jnp.int32, (N, N), 0) == lax.broadcasted_iota(
            jnp.int32, (N, N), 1
        )
        place = jnp.where(turned == 1, 1 - b, b) * N
        out[pl.ds(pl.multiple_of(place, N), N), :] = jnp.where(on_diag, -pot - hop, -hop)
    out[2 * N : 2 * N + 8, :] = vecs[...]


def row_times(vector, matrix):
    return jnp.dot(vector, matrix, precision=HIGHEST, preferred_element_type=jnp.float32)


def apply(vr, vi, gr, gi):
    both = jnp.concatenate([vr, vi, jnp.zeros((6, N), jnp.float32)], 0)
    a = row_times(both, gr)
    b = row_times(both, gi)
    return b[1:2] - a[0:1], -a[1:2] - b[0:1]


def load_block(ar, ai, real, link, energy):
    scale = outer_square(link)
    on_diag = lax.broadcasted_iota(jnp.int32, (N, N), 0) == lax.broadcasted_iota(
        jnp.int32, (N, N), 1
    )
    ar[...] = real + scale * ar[...] + jnp.where(on_diag, energy, 0.0)
    ai[...] = scale * ai[...] + jnp.where(on_diag, BROADENING, 0.0)


def outer_square(link):
    down = jnp.broadcast_to(link, (128, N)).T
    return jnp.concatenate([down, down], 1) * link


def eliminate(flag, energy, here, b, real, ar, ai, carry, mats, vecs, slot):
    pick = lambda i: jnp.where(b == 0, here[i : i + 1], here[i + 1 : i + 2])
    bond, src_r, src_i = pick(0), pick(2), pick(4)
    link = jnp.where(flag[0] == 1, bond, carry[3:4, :])
    load_block(ar, ai, real, link, energy[0])
    rhs_r = src_r + link * carry[0:1, :]
    rhs_i = src_i + link * carry[1:2, :]
    if mats is None:
        return link, bond, rhs_r, rhs_i
    invert(ar, ai)
    mats[slot, 0] = ar[...]
    mats[slot, 1] = ai[...]
    q_r, q_i = apply(rhs_r, rhs_i, ar[...], ai[...])
    now = jnp.concatenate([q_r, q_i, link, bond, jnp.zeros((4, N), jnp.float32)], 0)
    carry[...] = now
    vecs[slot] = now


def first_kernel(flag, energy, pack, mats, vecs, ar, ai, carry):
    ar[...] = jnp.zeros((N, N), jnp.float32)
    ai[...] = jnp.zeros((N, N), jnp.float32)
    carry[...] = jnp.zeros((8, N), jnp.float32)

    @pl.loop(0, 2)
    def _(b):
        real = pack[pl.ds(pl.multiple_of(b * N, N), N), :]
        here = pack[2 * N : 2 * N + 8, :]
        eliminate(flag, energy, here, b, real, ar, ai, carry, mats, vecs, b)


def middle_kernel(
    flag, energy, pack1, pack2, pack3, start, before, mats, vecs, ready, ar, ai, carry, hop, side
):
    ar[...] = start[1, 0]
    ai[...] = start[1, 1]
    carry[...] = before[1]
    for i, pack in enumerate((pack1, pack2, pack3)):
        hop[2 * i] = pack[0:N, :]
        hop[2 * i + 1] = pack[N : 2 * N, :]
        side[i] = pack[2 * N : 2 * N + 8, :]

    @pl.loop(0, 5)
    def _(j):
        b = lax.rem(j, 2)
        eliminate(flag, energy, side[j // 2], b, hop[j], ar, ai, carry, mats, vecs, j)

    link, bond, rhs_r, rhs_i = eliminate(
        flag, energy, side[2], 1, hop[5], ar, ai, carry, None, None, None
    )
    ready[0:N, :] = ar[...]
    ready[N : 2 * N, :] = ai[...]
    ready[2 * N : 2 * N + 8, :] = jnp.concatenate(
        [rhs_r, rhs_i, link, bond, jnp.zeros((4, N), jnp.float32)], 0
    )


def inner_kernel(ready, mat, vec, ar, ai):
    ar[...] = ready[0:N, :]
    ai[...] = ready[N : 2 * N, :]
    side = ready[2 * N : 2 * N + 8, :]
    invert(ar, ai)
    mat[0] = ar[...]
    mat[1] = ai[...]
    q_r, q_i = apply(side[0:1], side[1:2], ar[...], ai[...])
    vec[...] = jnp.concatenate([q_r, q_i, side[2:8]], 0)


def last_kernel(flag, weight, far, m0, v0, m1, v1, m7, v7, out, ar, ai):
    all_m = [m0.at[0], m0.at[1]] + [m1.at[j] for j in range(5)]
    all_v = [v0[0], v0[1]] + [v1[j] for j in range(5)]
    side = far[2 * N : 2 * N + 8, :]
    own = v7[...]
    middle = jnp.where(flag[0] == 1, side[3:4], own[3:4])
    scale = outer_square(middle)
    ar[...] = far[0:N, :] + scale * m7[0]
    ai[...] = far[N : 2 * N, :] + scale * m7[1]
    rhs_r = side[0:1] + middle * own[0:1]
    rhs_i = side[1:2] + middle * own[1:2]
    invert(ar, ai)
    now_r, now_i = apply(rhs_r, rhs_i, ar[...], ai[...])
    rows = []
    link = middle
    for mat, vec in [(m7, own)] + [(all_m[j], all_v[j]) for j in range(6, -1, -1)]:
        add_r, add_i = apply(link * now_r, link * now_i, mat[0], mat[1])
        now_r = vec[0:1] + add_r
        now_i = vec[1:2] + add_i
        rows.append(weight[0] * (now_r * now_r + now_i * now_i))
        link = vec[2:3]
    turned = flag[0] == 1
    low, high = rows[::-1], rows
    out[...] = jnp.where(turned, jnp.concatenate(high, 0), jnp.concatenate(low, 0))


SMEM = pl.BlockSpec(memory_space=pltpu.SMEM)
VMEM = pl.BlockSpec(memory_space=pltpu.VMEM)
PARAMS = pltpu.CompilerParams(vmem_limit_bytes=48 * 2**20)
MATRIX = pltpu.VMEM((N, N), jnp.float32)
SIDE = pltpu.VMEM((8, N), jnp.float32)


def shape(*dims):
    return jax.ShapeDtypeStruct(dims, jnp.float32)


def call(kernel, scalars, arrays, outs, scratch, steps=1):
    return pl.pallas_call(
        kernel,
        out_shape=outs,
        in_specs=[SMEM] * len(scalars) + [VMEM] * len(arrays),
        out_specs=jax.tree.map(lambda _: VMEM, outs),
        scratch_shapes=scratch,
        compiler_params=PARAMS,
        cost_estimate=pl.CostEstimate(
            flops=steps * 8 * N**3, bytes_accessed=steps * 4 * N * N, transcendentals=0
        ),
    )(*scalars, *arrays)


def shards(
    occupancy, onsite, defect_shift, site_order, lateral, coupling, energies, weights, sources
):
    slab = lax.axis_index("slab")
    column = lax.axis_index("energy")
    pot_piece = onsite + occupancy.astype(jnp.float32) * defect_shift
    mine = lax.dynamic_slice(site_order, (column * 16,), (16,))
    at = mine[:, None] == lax.broadcasted_iota(jnp.int32, (16, N), 1)
    spread = jnp.sum(jnp.where(at[None], pot_piece[:, :, None], 0.0), axis=1)
    piece = jnp.concatenate([lateral.reshape(32, N), spread, jnp.zeros((6, N), jnp.float32)], 0)
    got = lax.all_to_all(jnp.broadcast_to(piece[None], (16, 40, N)), "energy", 0, 0)
    flip = slab >= 4
    flag = flip.astype(jnp.int32)[None]
    vecs = jnp.stack([coupling, sources[0, 0], sources[1, 0]])
    vecs = jnp.where(flip, vecs[:, ::-1], vecs).reshape(6, N)
    vecs = jnp.concatenate([vecs, jnp.zeros((2, N), jnp.float32)], 0)
    own = call(prep_kernel, [flag], [got, vecs], shape(PACK, N), [])
    packs = [
        lax.ppermute(own, "slab", [(1, 0), (6, 7)]),
        lax.ppermute(own, "slab", [(2, 0), (5, 7)]),
        lax.ppermute(own, "slab", [(3, 0), (4, 7)]),
    ]
    scalars = [flag, energies]
    m0, v0 = call(
        first_kernel,
        scalars,
        [own],
        [shape(2, 2, N, N), shape(2, 8, N)],
        [MATRIX, MATRIX, SIDE],
        2,
    )
    m1, v1, ready = call(
        middle_kernel,
        scalars,
        packs + [m0, v0],
        [shape(5, 2, N, N), shape(5, 8, N), shape(PACK, N)],
        [MATRIX, MATRIX, SIDE, pltpu.VMEM((6, N, N), jnp.float32), pltpu.VMEM((3, 8, N), jnp.float32)],
        5,
    )
    far = lax.ppermute(ready, "slab", [(0, 7), (7, 0)])
    m7, v7 = call(
        inner_kernel, [], [ready], [shape(2, N, N), shape(8, N)], [MATRIX, MATRIX]
    )
    density = call(
        last_kernel,
        [flag, weights],
        [far, m0, v0, m1, v1, m7, v7],
        shape(8, N),
        [MATRIX, MATRIX],
    )
    parts = density.reshape(4, 2, 16, 16)
    low = jnp.where(slab == 0, parts, 0.0)
    high = jnp.where(slab == 7, parts, 0.0)
    sent = jnp.concatenate([low, high], 0).transpose(0, 2, 1, 3).reshape(128, 2, 16)
    return jnp.sum(lax.all_to_all(sent, ("slab", "energy"), 0, 0), axis=0)


def solution(mesh):
    return jax.shard_map(
        shards,
        mesh=mesh,
        in_specs=(
            P("slab", "energy"),
            P("slab", "energy"),
            P("slab", "energy"),
            P(),
            P("slab", "energy", None),
            P("slab", None),
            P("energy"),
            P("energy"),
            P(None, "energy", "slab", None),
        ),
        out_specs=P("slab", "energy"),
        check_vma=False,
    )
```

```python
import functools
import jax
import jax.numpy as jnp
from jax import lax
from jax.experimental import pallas as pl
from jax.experimental.pallas import tpu as pltpu
from jax.sharding import PartitionSpec as P

BROADENING = 1.2
LATERAL_SCALE = 0.9
HIGHEST = lax.Precision.HIGHEST
PACK = 2 * 256 + 8
N=256
W=32
S8=(8,128)
def row(t,s): return jnp.broadcast_to(t[s:s+1],S8)
def lane_of(t,idx): return jnp.take_along_axis(t,idx,axis=1)
def split3(x):
    h=x.astype(jnp.bfloat16); r=x-h.astype(jnp.float32)
    m=r.astype(jnp.bfloat16); l=(r-m.astype(jnp.float32)).astype(jnp.bfloat16)
    return h,m,l
MIX=True
def times(x,y): return (x[0]*y[0]-x[1]*y[1],x[0]*y[1]+x[1]*y[0])
def less(x,a,b): return (x[0]-(a[0]*b[0]-a[1]*b[1]),x[1]-(a[0]*b[1]+a[1]*b[0]))
def row2(x,j): return (row(x[0],j),row(x[1],j))
def panel(T,place,sub,lane):
    half=place//128; off=place-128*half
    nt=W//8
    Z=[]
    for s in range(nt):
        pick=lambda t: tuple(jnp.where(half==0,T[t][0][c],T[t][1][c]) for c in (0,1))
        idx=[jnp.full(S8,off+8*s+j,jnp.int32) for j in range(8)]
        wide=lambda x: [tuple(lane_of(c,idx[j]) for c in x) for j in range(8)]
        C=wide(pick(s))
        O={t:wide(pick(t)) for t in range(s+1,nt)}
        first=place+8*s
        for h in range(2):
            local=lane-(first-128*h)
            inside=(local>=0)&(local<8)
            minus=jnp.where(local==sub,-1.0,0.0)
            for t in range(s,nt):
                r,i=T[t][h]
                T[t][h]=(jnp.where(inside,minus if t==s else 0.0,r),jnp.where(inside,0.0,i))
        X=[T[s][0],T[s][1]]
        Q=None
        rows=[[],[]]
        p=row2(C[0],0)
        for j in range(8):
            inv=1.0/(p[0]*p[0]+p[1]*p[1])
            c=C[j]
            q=(p[0]*inv,-p[1]*inv)
            Q=q if j==0 else tuple(jnp.where(sub==j,a,b) for a,b in zip(q,Q))
            if j<7:
                e=row2(c,j+1)
                g=times(times(e,e),(p[0],-p[1]))
                n=row2(C[j+1],j+1)
                p=(n[0]-g[0]*inv,n[1]-g[1]*inv)
                low=tuple(jnp.where(sub>j,a,0.0) for a in c)
                scaled=times(c,q)
                for j2 in range(j+1,8):
                    w=row2(scaled,j2)
                    C[j2]=less(C[j2],low,w)
                    for t in range(s+1,min(nt,s+2) if MIX else nt): O[t][j2]=less(O[t][j2],O[t][j],w)
            for h in range(2):
                w=times(row2(X[h],j),q)
                rows[h].append(w)
                if j<7: X[h]=less(X[h],low,w)
        T[s]=X
        z=[times(x,Q) for x in X]
        Z.append(z)
        if s<nt-1:
            for h in range(2):
                x=T[s+1][h]
                for j in range(8): x=less(x,O[s+1][j],rows[h][j])
                T[s+1][h]=x
        if s<nt-2:
            if MIX:
                V=list(z)
                for j in range(7,0,-1):
                    u=times(C[j],Q)
                    u=tuple(jnp.where(sub<j,a,0.0) for a in u)
                    V=[less(v,u,row2(v,j)) for v in V]
                rows=[[row2(v,j) for j in range(8)] for v in V]
            for t in range(s+2,nt):
                for h in range(2):
                    x=T[t][h]
                    for j in range(8): x=less(x,O[t][j],rows[h][j])
                    T[t][h]=x
    for t in range(nt-1):
        for h in range(2):
            local=lane-(place-128*h)
            above=(local>=8*t+8)&(local<W)
            T[t][h]=tuple(jnp.where(above,0.0,x) for x in T[t][h])
            Z[t][h]=tuple(jnp.where(above,0.0,x) for x in Z[t][h])
    return T,Z
PR=((0,0),(0,1),(1,0),(1,1),(0,2),(2,0))
def invert(ar,ai):
    sub=lax.broadcasted_iota(jnp.int32,S8,0); lane=lax.broadcasted_iota(jnp.int32,S8,1)
    @pl.loop(0,N//W)
    def _(k):
        place=pl.multiple_of(k*W,W)
        old=[ar[pl.ds(place,W),:],ai[pl.ds(place,W),:]]
        T=[[tuple(old[c][8*t:8*t+8,128*h:128*h+128] for c in (0,1)) for h in (0,1)] for t in range(W//8)]
        Y,Z=panel(T,place,sub,lane)
        whole=lambda M: [jnp.concatenate([jnp.concatenate([m[0][c],m[1][c]],1) for m in M],0) for c in (0,1)]
        ys=[split3(u) for u in whole(Y)]; zs=[split3(v) for v in whole(Z)]; ns=[-v for v in zs[1]]
        left=jnp.concatenate([ys[0][a] for a,_ in PR]+[ys[1][a] for a,_ in PR],0)
        re=jnp.concatenate([zs[0][b] for _,b in PR]+[ns[b] for _,b in PR],0)
        im=jnp.concatenate([zs[1][b] for _,b in PR]+[zs[0][b] for _,b in PR],0)
        right=jnp.concatenate([re,im],1)
        out=lax.dot_general(left,right,(((0,),(0,)),((),())),preferred_element_type=jnp.float32)
        full=lax.broadcasted_iota(jnp.int32,(1,N),1)-place
        keep=jnp.broadcast_to((full<0)|(full>=W),(N,N))
        ar[pl.ds(place,W),:]=jnp.zeros((W,N),jnp.float32)
        ai[pl.ds(place,W),:]=jnp.zeros((W,N),jnp.float32)
        ar[...]=jnp.where(keep,ar[...],0.0)-out[:,:N]
        ai[...]=jnp.where(keep,ai[...],0.0)-out[:,N:]


def prep_kernel(flag, got, vecs, out):
    turned = flag[0]
    for b in range(2):
        rows = jnp.concatenate([got[e, 16 * b : 16 * b + 16, :] for e in range(16)], 0)
        hop = LATERAL_SCALE * (rows + rows.T)
        pot = got[0, 32 + b : 33 + b, :]
        for e in range(1, 16):
            pot = pot + got[e, 32 + b : 33 + b, :]
        on_diag = lax.broadcasted_iota(jnp.int32, (N, N), 0) == lax.broadcasted_iota(
            jnp.int32, (N, N), 1
        )
        place = jnp.where(turned == 1, 1 - b, b) * N
        out[pl.ds(pl.multiple_of(place, N), N), :] = jnp.where(on_diag, -pot - hop, -hop)
    out[2 * N : 2 * N + 8, :] = vecs[...]


def row_times(vector, matrix, turned=False):
    return lax.dot_general(
        vector,
        matrix,
        (((1,), (1 if turned else 0,)), ((), ())),
        precision=HIGHEST,
        preferred_element_type=jnp.float32,
    )


def apply(v, gr, gi, turned=False):
    both = jnp.concatenate([v[0], v[1], jnp.zeros((6, N), jnp.float32)], 0)
    a = row_times(both, gr, turned)
    b = row_times(both, gi, turned)
    return a[0:1] - b[1:2], a[1:2] + b[0:1]


def product(a, b, turned=False):
    axis = 0 if turned else 1
    a3 = [split3(a[0]), split3(a[1])]
    b3 = [split3(b[0]), split3(b[1])]
    out_r = out_i = 0.0
    for i, j in PR[::-1]:
        left = jnp.concatenate([a3[0][i], a3[1][i]], axis)
        right = jnp.concatenate(
            [
                jnp.concatenate([b3[0][j], b3[1][j]], 1),
                jnp.concatenate([-b3[1][j], b3[0][j]], 1),
            ],
            0,
        )
        out = lax.dot_general(
            left, right, (((axis,), (0,)), ((), ())), preferred_element_type=jnp.float32
        )
        out_r = out_r + out[:, :N]
        out_i = out_i + out[:, N:]
    return out_r, out_i


def on_diagonal():
    return lax.broadcasted_iota(jnp.int32, (N, N), 0) == lax.broadcasted_iota(
        jnp.int32, (N, N), 1
    )


def down(link):
    tall = jnp.broadcast_to(link, (128, N)).T
    return jnp.concatenate([tall, tall], 1)


def load_block(ar, ai, real, link, energy):
    scale = down(link) * link
    diag = on_diagonal()
    ar[...] = real + scale * ar[...] + jnp.where(diag, energy, 0.0)
    ai[...] = scale * ai[...] + jnp.where(diag, BROADENING, 0.0)


def eliminate(flag, energy, bond, source, real, ar, ai, carry, mats, vecs, slot):
    link = jnp.where(flag[0] == 1, bond, carry[3:4, :])
    load_block(ar, ai, real, link, energy[0])
    rhs = (source[0] + link * carry[0:1, :], source[1] + link * carry[1:2, :])
    invert(ar, ai)
    mats[slot, 0] = ar[...]
    mats[slot, 1] = ai[...]
    q_r, q_i = apply(rhs, ar[...], ai[...])
    now = jnp.concatenate([-q_r, -q_i, link, bond, jnp.zeros((4, N), jnp.float32)], 0)
    carry[...] = now
    vecs[slot] = now


def fold(one, two):
    row_id = lax.broadcasted_iota(jnp.int32, (N, N), 0)
    lane_id = lax.broadcasted_iota(jnp.int32, (N, N), 1)
    diag = jnp.sum(jnp.where(row_id == lane_id, two, 0.0), axis=0, keepdims=True)
    return jnp.where(row_id >= lane_id, one, two), diag


def unfold(both, diag):
    row_id = lax.broadcasted_iota(jnp.int32, (N, N), 0)
    lane_id = lax.broadcasted_iota(jnp.int32, (N, N), 1)
    other = both.T
    one = jnp.where(row_id >= lane_id, both, other)
    two = jnp.where(row_id < lane_id, both, jnp.where(row_id == lane_id, diag, other))
    return one, two


def first_kernel(flag, inner, energy, own, after, mats, vecs, mid, ar, ai, carry, hop, side):
    ar[...] = jnp.zeros((N, N), jnp.float32)
    ai[...] = jnp.zeros((N, N), jnp.float32)
    carry[...] = jnp.zeros((8, N), jnp.float32)
    first = own[2 * N : 2 * N + 8, :]
    second = after[2 * N : 2 * N + 8, :]
    is_inner = inner[0] == 1
    hop[0] = jnp.where(is_inner, own[N : 2 * N, :], own[0:N, :])
    hop[1] = jnp.where(is_inner, after[0:N, :], own[N : 2 * N, :])
    rows = lambda m, b: jnp.concatenate([m[b : b + 1], m[2 + b : 3 + b], m[4 + b : 5 + b]] * 2, 0)
    side[0, 0:6] = jnp.where(is_inner, rows(first, 1), rows(first, 0))
    side[1, 0:6] = jnp.where(is_inner, rows(second, 0), rows(first, 1))

    @pl.loop(0, 2)
    def _(b):
        here = side[b]
        eliminate(
            flag, energy, here[0:1], (here[1:2], here[2:3]), hop[b], ar, ai, carry, mats, vecs, b
        )

    @pl.when(is_inner)
    def _():
        link = carry[2:3, :]
        n5 = (mats[0, 0], mats[0, 1])
        n6 = (mats[1, 0], mats[1, 1])
        m56 = product((n5[0] * link, n5[1] * link), n6)
        m55 = product((m56[0] * link, m56[1] * link), n5)
        m55 = (-n5[0] - m55[0], -n5[1] - m55[1])
        m66 = (-n6[0], -n6[1])
        folded = [fold(*m55), fold(*m66), fold(own[0:N, :], after[N : 2 * N, :])]
        mid[0:N, :] = m56[0]
        mid[N : 2 * N, :] = m56[1]
        for i in range(3):
            mid[(2 + i) * N : (3 + i) * N, :] = folded[i][0]
        s5 = (side[0, 1:2, :], side[0, 2:3, :])
        s6 = (side[1, 1:2, :], side[1, 2:3, :])
        a = apply(s5, *m55)
        b = apply(s6, *m56, turned=True)
        c = apply(s5, *m56)
        d = apply(s6, *m66)
        zero = jnp.zeros((1, N), jnp.float32)
        mid[5 * N : 5 * N + 8, :] = jnp.concatenate(
            [a[0] + b[0], a[1] + b[1], c[0] + d[0], c[1] + d[1]]
            + [folded[i][1] for i in range(3)]
            + [zero],
            0,
        )
        mid[5 * N + 8 : 5 * N + 16, :] = first
        mid[5 * N + 16 : 5 * N + 24, :] = second


def second_kernel(flag, energy, after, start, before, mats, vecs, ar, ai, carry, side):
    ar[...] = start[1, 0]
    ai[...] = start[1, 1]
    carry[...] = before[1]
    have = after[2 * N : 2 * N + 8, :]
    for b in range(2):
        side[b, 0:3] = jnp.concatenate(
            [have[b : b + 1], have[2 + b : 3 + b], have[4 + b : 5 + b]], 0
        )

    @pl.loop(0, 2)
    def _(b):
        here = side[b]
        real = after[pl.ds(pl.multiple_of(b * N, N), N), :]
        eliminate(
            flag, energy, here[0:1], (here[1:2], here[2:3]), real, ar, ai, carry, mats, vecs, b
        )


def third_kernel(flag, energy, start, before, mid, mat, vec, ready, ar, ai):
    p2 = mid[5 * N + 8 : 5 * N + 16, :]
    p3 = mid[5 * N + 16 : 5 * N + 24, :]
    back = flag[0] == 1
    link = jnp.where(back, p2[0:1], before[1, 3:4, :])
    c4 = jnp.where(back, p2[1:2], p2[0:1])
    c6 = jnp.where(back, p3[1:2], p3[0:1])
    t = mid[5 * N : 5 * N + 8, :]
    ar[...] = start[1, 0]
    ai[...] = start[1, 1]
    a4, a7 = unfold(mid[4 * N : 5 * N, :], t[6:7])
    m55 = unfold(mid[2 * N : 3 * N, :], t[4:5])
    m66 = unfold(mid[3 * N : 4 * N, :], t[5:6])
    load_block(ar, ai, a4, link, energy[0])
    down4 = down(c4)
    square = down4 * c4
    ar[...] = ar[...] - square * m55[0]
    ai[...] = ai[...] - square * m55[1]
    rhs = (
        p2[2:3] + link * before[1, 0:1, :] + c4 * t[0:1],
        p2[4:5] + link * before[1, 1:2, :] + c4 * t[1:2],
    )
    invert(ar, ai)
    mat[0] = ar[...]
    mat[1] = ai[...]
    n_r, n_i = apply(rhs, ar[...], ai[...])
    q = (-n_r, -n_i)
    vec[...] = jnp.concatenate([q[0], q[1], link, c4, c6, jnp.zeros((3, N), jnp.float32)], 0)
    cross = down4 * c6
    ready[0:N, :] = cross * mid[0:N, :]
    ready[N : 2 * N, :] = cross * mid[N : 2 * N, :]
    k = (ready[0:N, :], ready[N : 2 * N, :])
    x = product((ar[...], ai[...]), k)
    y = product(k, x, turned=True)
    onto = apply(q, *k)
    square = down(c6) * c6
    diag = on_diagonal()
    ready[0:N, :] = (
        a7 + jnp.where(diag, energy[0], 0.0) - square * m66[0] + y[0]
    )
    ready[N : 2 * N, :] = (
        jnp.where(diag, BROADENING, 0.0) - square * m66[1] + y[1]
    )
    ready[2 * N : 2 * N + 8, :] = jnp.concatenate(
        [
            p3[3:4] + c6 * t[2:3] + onto[0],
            p3[5:6] + c6 * t[3:4] + onto[1],
            link,
            p3[1:2],
            jnp.zeros((4, N), jnp.float32),
        ],
        0,
    )


def inner_kernel(ready, mat, vec, ar, ai):
    ar[...] = ready[0:N, :]
    ai[...] = ready[N : 2 * N, :]
    side = ready[2 * N : 2 * N + 8, :]
    invert(ar, ai)
    mat[0] = ar[...]
    mat[1] = ai[...]
    q_r, q_i = apply((side[0:1], side[1:2]), ar[...], ai[...])
    vec[...] = jnp.concatenate([-q_r, -q_i, side[2:8]], 0)


def last_kernel(flag, weight, far, m0, v0, m1, v1, m4, v4, m7, v7, mid, out, ar, ai):
    side = far[2 * N : 2 * N + 8, :]
    own = v7[...]
    middle = jnp.where(flag[0] == 1, side[3:4], own[3:4])
    scale = down(middle) * middle
    ar[...] = far[0:N, :] + scale * m7[0]
    ai[...] = far[N : 2 * N, :] + scale * m7[1]
    rhs = (side[0:1] + middle * own[0:1], side[1:2] + middle * own[1:2])
    invert(ar, ai)
    v_r, v_i = apply(rhs, ar[...], ai[...])
    psi = {8: (-v_r, -v_i)}
    scaled = lambda c, v: (c * v[0], c * v[1])

    def back(q, link, later, mat_r, mat_i):
        add = apply(scaled(link, later), mat_r, mat_i)
        return q[0:1] - add[0], q[1:2] - add[1]

    psi[7] = back(own, middle, psi[8], m7[0], m7[1])
    four = v4[...]
    c4, c6 = four[3:4], four[4:5]
    t = mid[5 * N : 5 * N + 8, :]
    right = scaled(c6, psi[7])
    w = apply(right, mid[0:N, :], mid[N : 2 * N, :], turned=True)
    psi[4] = back(four, c4, w, m4[0], m4[1])
    left = scaled(c4, psi[4])
    a = apply(left, *unfold(mid[2 * N : 3 * N, :], t[4:5]))
    psi[5] = (t[0:1] + a[0] + w[0], t[1:2] + a[1] + w[1])
    b = apply(left, mid[0:N, :], mid[N : 2 * N, :])
    c = apply(right, *unfold(mid[3 * N : 4 * N, :], t[5:6]))
    psi[6] = (t[2:3] + b[0] + c[0], t[3:4] + b[1] + c[1])
    psi[3] = back(v1[1], four[2:3], psi[4], m1[1, 0], m1[1, 1])
    psi[2] = back(v1[0], v1[1, 2:3, :], psi[3], m1[0, 0], m1[0, 1])
    psi[1] = back(v0[1], v1[0, 2:3, :], psi[2], m0[1, 0], m0[1, 1])
    psi[0] = back(v0[0], v0[1, 2:3, :], psi[1], m0[0, 0], m0[0, 1])
    rows = [weight[0] * (psi[j][0] * psi[j][0] + psi[j][1] * psi[j][1]) for j in range(8)]
    out[...] = jnp.where(
        flag[0] == 1, jnp.concatenate(rows[::-1], 0), jnp.concatenate(rows, 0)
    )


SMEM = pl.BlockSpec(memory_space=pltpu.SMEM)
VMEM = pl.BlockSpec(memory_space=pltpu.VMEM)
PARAMS = pltpu.CompilerParams(vmem_limit_bytes=48 * 2**20)
MATRIX = pltpu.VMEM((N, N), jnp.float32)
SIDE = pltpu.VMEM((8, N), jnp.float32)


def shape(*dims):
    return jax.ShapeDtypeStruct(dims, jnp.float32)


def call(kernel, scalars, arrays, outs, scratch, steps=1):
    return pl.pallas_call(
        kernel,
        out_shape=outs,
        in_specs=[SMEM] * len(scalars) + [VMEM] * len(arrays),
        out_specs=jax.tree.map(lambda _: VMEM, outs),
        scratch_shapes=scratch,
        compiler_params=PARAMS,
        cost_estimate=pl.CostEstimate(
            flops=steps * 8 * N**3, bytes_accessed=steps * 4 * N * N, transcendentals=0
        ),
    )(*scalars, *arrays)


def shards(
    occupancy, onsite, defect_shift, site_order, lateral, coupling, energies, weights, sources
):
    slab = lax.axis_index("slab")
    column = lax.axis_index("energy")
    pot_piece = onsite + occupancy.astype(jnp.float32) * defect_shift
    mine = lax.dynamic_slice(site_order, (column * 16,), (16,))
    at = mine[:, None] == lax.broadcasted_iota(jnp.int32, (16, N), 1)
    spread = jnp.sum(jnp.where(at[None], pot_piece[:, :, None], 0.0), axis=1)
    piece = jnp.concatenate([lateral.reshape(32, N), spread, jnp.zeros((6, N), jnp.float32)], 0)
    got = lax.all_to_all(jnp.broadcast_to(piece[None], (16, 40, N)), "energy", 0, 0)
    flip = slab >= 4
    flag = flip.astype(jnp.int32)[None]
    vecs = jnp.stack([coupling, sources[0, 0], sources[1, 0]])
    vecs = jnp.where(flip, vecs[:, ::-1], vecs).reshape(6, N)
    vecs = jnp.concatenate([vecs, jnp.zeros((2, N), jnp.float32)], 0)
    own = call(prep_kernel, [flag], [got, vecs], shape(PACK, N), [])
    after = lax.ppermute(own, "slab", [(1, 0), (6, 7), (3, 2), (4, 5)])
    inner = ((slab == 2) | (slab == 5)).astype(jnp.int32)[None]
    pair = [shape(2, 2, N, N), shape(2, 8, N)]
    square = [shape(2, N, N), shape(8, N)]
    room = [MATRIX, MATRIX]
    sides = pltpu.VMEM((2, 8, N), jnp.float32)
    m0, v0, mid = call(
        first_kernel,
        [flag, inner, energies],
        [own, after],
        pair + [shape(5 * N + 24, N)],
        room + [SIDE, pltpu.VMEM((2, N, N), jnp.float32), sides],
        2,
    )
    mid = lax.ppermute(mid, "slab", [(2, 0), (5, 7)])
    m1, v1 = call(
        second_kernel, [flag, energies], [after, m0, v0], pair, room + [SIDE, sides], 2
    )
    m4, v4, ready = call(
        third_kernel,
        [flag, energies],
        [m1, v1, mid],
        square + [shape(PACK, N)],
        room,
    )
    far = lax.ppermute(ready, "slab", [(0, 7), (7, 0)])
    m7, v7 = call(inner_kernel, [], [ready], square, room)
    density = call(
        last_kernel,
        [flag, weights],
        [far, m0, v0, m1, v1, m4, v4, m7, v7, mid],
        shape(8, N),
        room,
    )
    parts = density.reshape(4, 2, 16, 16)
    low = jnp.where(slab == 0, parts, 0.0)
    high = jnp.where(slab == 7, parts, 0.0)
    sent = jnp.concatenate([low, high], 0).transpose(0, 2, 1, 3).reshape(128, 2, 16)
    return jnp.sum(lax.all_to_all(sent, ("slab", "energy"), 0, 0), axis=0)


def solution(mesh):
    return jax.shard_map(
        shards,
        mesh=mesh,
        in_specs=(
            P("slab", "energy"),
            P("slab", "energy"),
            P("slab", "energy"),
            P(),
            P("slab", "energy", None),
            P("slab", None),
            P("energy"),
            P("energy"),
            P(None, "energy", "slab", None),
        ),
        out_specs=P("slab", "energy"),
        check_vma=False,
    )
```

```python
import functools
import jax
import jax.numpy as jnp
from jax import lax
from jax.experimental import pallas as pl
from jax.experimental.pallas import tpu as pltpu
from jax.sharding import PartitionSpec as P

BROADENING = 1.2
LATERAL_SCALE = 0.9
HIGHEST = lax.Precision.HIGHEST
PACK = 2 * 256 + 8
N=256
W=32
S8=(8,128)
def row(t,s): return jnp.broadcast_to(t[s:s+1],S8)
def lane_of(t,idx): return jnp.take_along_axis(t,idx,axis=1)
def split3(x):
    h=x.astype(jnp.bfloat16); r=x-h.astype(jnp.float32)
    m=r.astype(jnp.bfloat16); l=(r-m.astype(jnp.float32)).astype(jnp.bfloat16)
    return h,m,l
MIX=True
def times(x,y): return (x[0]*y[0]-x[1]*y[1],x[0]*y[1]+x[1]*y[0])
def less(x,a,b): return (x[0]-(a[0]*b[0]-a[1]*b[1]),x[1]-(a[0]*b[1]+a[1]*b[0]))
def row2(x,j): return (row(x[0],j),row(x[1],j))
def panel(T,place,sub,lane):
    half=place//128; off=place-128*half
    nt=W//8
    Z=[]
    for s in range(nt):
        pick=lambda t: tuple(jnp.where(half==0,T[t][0][c],T[t][1][c]) for c in (0,1))
        idx=[jnp.full(S8,off+8*s+j,jnp.int32) for j in range(8)]
        wide=lambda x: [tuple(lane_of(c,idx[j]) for c in x) for j in range(8)]
        C=wide(pick(s))
        O={t:wide(pick(t)) for t in range(s+1,nt)}
        first=place+8*s
        for h in range(2):
            local=lane-(first-128*h)
            inside=(local>=0)&(local<8)
            minus=jnp.where(local==sub,-1.0,0.0)
            for t in range(s,nt):
                r,i=T[t][h]
                T[t][h]=(jnp.where(inside,minus if t==s else 0.0,r),jnp.where(inside,0.0,i))
        X=[T[s][0],T[s][1]]
        Q=None
        rows=[[],[]]
        p=row2(C[0],0)
        for j in range(8):
            inv=1.0/(p[0]*p[0]+p[1]*p[1])
            c=C[j]
            q=(p[0]*inv,-p[1]*inv)
            Q=q if j==0 else tuple(jnp.where(sub==j,a,b) for a,b in zip(q,Q))
            if j<7:
                e=row2(c,j+1)
                g=times(times(e,e),(p[0],-p[1]))
                n=row2(C[j+1],j+1)
                p=(n[0]-g[0]*inv,n[1]-g[1]*inv)
                low=tuple(jnp.where(sub>j,a,0.0) for a in c)
                scaled=times(c,q)
                for j2 in range(j+1,8):
                    w=row2(scaled,j2)
                    C[j2]=less(C[j2],low,w)
                    for t in range(s+1,min(nt,s+2) if MIX else nt): O[t][j2]=less(O[t][j2],O[t][j],w)
            for h in range(2):
                w=times(row2(X[h],j),q)
                rows[h].append(w)
                if j<7: X[h]=less(X[h],low,w)
        T[s]=X
        z=[times(x,Q) for x in X]
        Z.append(z)
        if s<nt-1:
            for h in range(2):
                x=T[s+1][h]
                for j in range(8): x=less(x,O[s+1][j],rows[h][j])
                T[s+1][h]=x
        if s<nt-2:
            if MIX:
                V=list(z)
                for j in range(7,0,-1):
                    u=times(C[j],Q)
                    u=tuple(jnp.where(sub<j,a,0.0) for a in u)
                    V=[less(v,u,row2(v,j)) for v in V]
                rows=[[row2(v,j) for j in range(8)] for v in V]
            for t in range(s+2,nt):
                for h in range(2):
                    x=T[t][h]
                    for j in range(8): x=less(x,O[t][j],rows[h][j])
                    T[t][h]=x
    for t in range(nt-1):
        for h in range(2):
            local=lane-(place-128*h)
            above=(local>=8*t+8)&(local<W)
            T[t][h]=tuple(jnp.where(above,0.0,x) for x in T[t][h])
            Z[t][h]=tuple(jnp.where(above,0.0,x) for x in Z[t][h])
    return T,Z
PR=((0,0),(0,1),(1,0),(1,1),(0,2),(2,0))
def invert(ar,ai):
    sub=lax.broadcasted_iota(jnp.int32,S8,0); lane=lax.broadcasted_iota(jnp.int32,S8,1)
    @pl.loop(0,N//W)
    def _(k):
        place=pl.multiple_of(k*W,W)
        old=[ar[pl.ds(place,W),:],ai[pl.ds(place,W),:]]
        T=[[tuple(old[c][8*t:8*t+8,128*h:128*h+128] for c in (0,1)) for h in (0,1)] for t in range(W//8)]
        Y,Z=panel(T,place,sub,lane)
        whole=lambda M: [jnp.concatenate([jnp.concatenate([m[0][c],m[1][c]],1) for m in M],0) for c in (0,1)]
        ys=[split3(u) for u in whole(Y)]; zs=[split3(v) for v in whole(Z)]; ns=[-v for v in zs[1]]
        left=jnp.concatenate([ys[0][a] for a,_ in PR]+[ys[1][a] for a,_ in PR],0)
        re=jnp.concatenate([zs[0][b] for _,b in PR]+[ns[b] for _,b in PR],0)
        im=jnp.concatenate([zs[1][b] for _,b in PR]+[zs[0][b] for _,b in PR],0)
        right=jnp.concatenate([re,im],1)
        out=lax.dot_general(left,right,(((0,),(0,)),((),())),preferred_element_type=jnp.float32)
        full=lax.broadcasted_iota(jnp.int32,(1,N),1)-place
        keep=jnp.broadcast_to((full<0)|(full>=W),(N,N))
        ar[pl.ds(place,W),:]=jnp.zeros((W,N),jnp.float32)
        ai[pl.ds(place,W),:]=jnp.zeros((W,N),jnp.float32)
        ar[...]=jnp.where(keep,ar[...],0.0)-out[:,:N]
        ai[...]=jnp.where(keep,ai[...],0.0)-out[:,N:]


def prep_kernel(flag, got, vecs, out):
    turned = flag[0]
    for b in range(2):
        rows = jnp.concatenate([got[e, 16 * b : 16 * b + 16, :] for e in range(16)], 0)
        hop = LATERAL_SCALE * (rows + rows.T)
        pot = got[0, 32 + b : 33 + b, :]
        for e in range(1, 16):
            pot = pot + got[e, 32 + b : 33 + b, :]
        on_diag = lax.broadcasted_iota(jnp.int32, (N, N), 0) == lax.broadcasted_iota(
            jnp.int32, (N, N), 1
        )
        place = jnp.where(turned == 1, 1 - b, b) * N
        out[pl.ds(pl.multiple_of(place, N), N), :] = jnp.where(on_diag, -pot - hop, -hop)
    out[2 * N : 2 * N + 8, :] = vecs[...]


def row_times(vector, matrix, turned=False):
    return lax.dot_general(
        vector,
        matrix,
        (((1,), (1 if turned else 0,)), ((), ())),
        precision=HIGHEST,
        preferred_element_type=jnp.float32,
    )


def apply(v, gr, gi, turned=False):
    if not turned:
        tall = [jnp.broadcast_to(x, (128, N)).T for x in v]
        halves = [[], []]
        for h in range(0, N, 128):
            a, b = gr[:, h : h + 128], gi[:, h : h + 128]
            halves[0].append(jnp.sum(tall[0] * a - tall[1] * b, axis=0, keepdims=True))
            halves[1].append(jnp.sum(tall[0] * b + tall[1] * a, axis=0, keepdims=True))
        return jnp.concatenate(halves[0], 1), jnp.concatenate(halves[1], 1)
    both = jnp.concatenate([v[0], v[1], jnp.zeros((6, N), jnp.float32)], 0)
    a = row_times(both, gr, turned)
    b = row_times(both, gi, turned)
    return a[0:1] - b[1:2], a[1:2] + b[0:1]


def product(a, b, turned=False):
    axis = 0 if turned else 1
    a3 = [split3(a[0]), split3(a[1])]
    b3 = [split3(b[0]), split3(b[1])]
    out_r = out_i = 0.0
    for i, j in PR[::-1]:
        left = jnp.concatenate([a3[0][i], a3[1][i]], axis)
        right = jnp.concatenate(
            [
                jnp.concatenate([b3[0][j], b3[1][j]], 1),
                jnp.concatenate([-b3[1][j], b3[0][j]], 1),
            ],
            0,
        )
        out = lax.dot_general(
            left, right, (((axis,), (0,)), ((), ())), preferred_element_type=jnp.float32
        )
        out_r = out_r + out[:, :N]
        out_i = out_i + out[:, N:]
    return out_r, out_i


def on_diagonal():
    return lax.broadcasted_iota(jnp.int32, (N, N), 0) == lax.broadcasted_iota(
        jnp.int32, (N, N), 1
    )


def down(link):
    tall = jnp.broadcast_to(link, (128, N)).T
    return jnp.concatenate([tall, tall], 1)


def load_block(ar, ai, real, link, energy):
    scale = down(link) * link
    diag = on_diagonal()
    ar[...] = real + scale * ar[...] + jnp.where(diag, energy, 0.0)
    ai[...] = scale * ai[...] + jnp.where(diag, BROADENING, 0.0)


def eliminate(flag, energy, bond, source, real, ar, ai, carry, mats, vecs, slot):
    link = jnp.where(flag[0] == 1, bond, carry[3:4, :])
    load_block(ar, ai, real, link, energy[0])
    rhs = (source[0] + link * carry[0:1, :], source[1] + link * carry[1:2, :])
    invert(ar, ai)
    mats[slot, 0] = ar[...]
    mats[slot, 1] = ai[...]
    q_r, q_i = apply(rhs, ar[...], ai[...])
    now = jnp.concatenate([-q_r, -q_i, link, bond, jnp.zeros((4, N), jnp.float32)], 0)
    carry[...] = now
    vecs[slot] = now


def fold(one, two):
    row_id = lax.broadcasted_iota(jnp.int32, (N, N), 0)
    lane_id = lax.broadcasted_iota(jnp.int32, (N, N), 1)
    diag = jnp.sum(jnp.where(row_id == lane_id, two, 0.0), axis=0, keepdims=True)
    return jnp.where(row_id >= lane_id, one, two), diag


def unfold(both, diag):
    row_id = lax.broadcasted_iota(jnp.int32, (N, N), 0)
    lane_id = lax.broadcasted_iota(jnp.int32, (N, N), 1)
    other = both.T
    one = jnp.where(row_id >= lane_id, both, other)
    two = jnp.where(row_id < lane_id, both, jnp.where(row_id == lane_id, diag, other))
    return one, two


def first_kernel(flag, inner, energy, own, after, mats, vecs, mid, kept, ar, ai, carry, hop, side):
    ar[...] = jnp.zeros((N, N), jnp.float32)
    ai[...] = jnp.zeros((N, N), jnp.float32)
    carry[...] = jnp.zeros((8, N), jnp.float32)
    first = own[2 * N : 2 * N + 8, :]
    second = after[2 * N : 2 * N + 8, :]
    is_inner = inner[0] == 1
    kept[...] = after[...]
    hop[0] = jnp.where(is_inner, own[N : 2 * N, :], own[0:N, :])
    hop[1] = jnp.where(is_inner, after[0:N, :], own[N : 2 * N, :])
    rows = lambda m, b: jnp.concatenate([m[b : b + 1], m[2 + b : 3 + b], m[4 + b : 5 + b]] * 2, 0)
    side[0, 0:6] = jnp.where(is_inner, rows(first, 1), rows(first, 0))
    side[1, 0:6] = jnp.where(is_inner, rows(second, 0), rows(first, 1))

    @pl.loop(0, 2)
    def _(b):
        here = side[b]
        eliminate(
            flag, energy, here[0:1], (here[1:2], here[2:3]), hop[b], ar, ai, carry, mats, vecs, b
        )

    @pl.when(is_inner)
    def _():
        link = carry[2:3, :]
        n5 = (mats[0, 0], mats[0, 1])
        n6 = (mats[1, 0], mats[1, 1])
        m56 = product((n5[0] * link, n5[1] * link), n6)
        m55 = product((m56[0] * link, m56[1] * link), n5)
        m55 = (-n5[0] - m55[0], -n5[1] - m55[1])
        m66 = (-n6[0], -n6[1])
        folded = [fold(*m55), fold(*m66), fold(own[0:N, :], after[N : 2 * N, :])]
        mid[0:N, :] = m56[0]
        mid[N : 2 * N, :] = m56[1]
        for i in range(3):
            mid[(2 + i) * N : (3 + i) * N, :] = folded[i][0]
        s5 = (side[0, 1:2, :], side[0, 2:3, :])
        s6 = (side[1, 1:2, :], side[1, 2:3, :])
        a = apply(s5, *m55)
        b = apply(s6, *m56, turned=True)
        c = apply(s5, *m56)
        d = apply(s6, *m66)
        zero = jnp.zeros((1, N), jnp.float32)
        mid[5 * N : 5 * N + 8, :] = jnp.concatenate(
            [a[0] + b[0], a[1] + b[1], c[0] + d[0], c[1] + d[1]]
            + [folded[i][1] for i in range(3)]
            + [zero],
            0,
        )
        mid[5 * N + 8 : 5 * N + 16, :] = first
        mid[5 * N + 16 : 5 * N + 24, :] = second


def second_kernel(flag, energy, after, start, before, mats, vecs, ar, ai, carry, side):
    ar[...] = start[1, 0]
    ai[...] = start[1, 1]
    carry[...] = before[1]
    have = after[2 * N : 2 * N + 8, :]
    for b in range(2):
        side[b, 0:3] = jnp.concatenate(
            [have[b : b + 1], have[2 + b : 3 + b], have[4 + b : 5 + b]], 0
        )

    @pl.loop(0, 2)
    def _(b):
        here = side[b]
        real = after[pl.ds(pl.multiple_of(b * N, N), N), :]
        eliminate(
            flag, energy, here[0:1], (here[1:2], here[2:3]), real, ar, ai, carry, mats, vecs, b
        )


def third_kernel(flag, energy, start, before, mid, mat, vec, ready, ar, ai):
    p2 = mid[5 * N + 8 : 5 * N + 16, :]
    p3 = mid[5 * N + 16 : 5 * N + 24, :]
    back = flag[0] == 1
    link = jnp.where(back, p2[0:1], before[1, 3:4, :])
    c4 = jnp.where(back, p2[1:2], p2[0:1])
    c6 = jnp.where(back, p3[1:2], p3[0:1])
    t = mid[5 * N : 5 * N + 8, :]
    ar[...] = start[1, 0]
    ai[...] = start[1, 1]
    a4, a7 = unfold(mid[4 * N : 5 * N, :], t[6:7])
    m55 = unfold(mid[2 * N : 3 * N, :], t[4:5])
    m66 = unfold(mid[3 * N : 4 * N, :], t[5:6])
    load_block(ar, ai, a4, link, energy[0])
    down4 = down(c4)
    square = down4 * c4
    ar[...] = ar[...] - square * m55[0]
    ai[...] = ai[...] - square * m55[1]
    rhs = (
        p2[2:3] + link * before[1, 0:1, :] + c4 * t[0:1],
        p2[4:5] + link * before[1, 1:2, :] + c4 * t[1:2],
    )
    invert(ar, ai)
    mat[0] = ar[...]
    mat[1] = ai[...]
    n_r, n_i = apply(rhs, ar[...], ai[...])
    q = (-n_r, -n_i)
    vec[...] = jnp.concatenate([q[0], q[1], link, c4, c6, jnp.zeros((3, N), jnp.float32)], 0)
    cross = down4 * c6
    ready[0:N, :] = cross * mid[0:N, :]
    ready[N : 2 * N, :] = cross * mid[N : 2 * N, :]
    k = (ready[0:N, :], ready[N : 2 * N, :])
    x = product((ar[...], ai[...]), k)
    y = product(k, x, turned=True)
    onto = apply(q, *k)
    square = down(c6) * c6
    diag = on_diagonal()
    ready[0:N, :] = (
        a7 + jnp.where(diag, energy[0], 0.0) - square * m66[0] + y[0]
    )
    ready[N : 2 * N, :] = (
        jnp.where(diag, BROADENING, 0.0) - square * m66[1] + y[1]
    )
    ready[2 * N : 2 * N + 8, :] = jnp.concatenate(
        [
            p3[3:4] + c6 * t[2:3] + onto[0],
            p3[5:6] + c6 * t[3:4] + onto[1],
            link,
            p3[1:2],
            jnp.zeros((4, N), jnp.float32),
        ],
        0,
    )


def inner_kernel(ready, four, mat, vec, held, ar, ai):
    ar[...] = ready[0:N, :]
    ai[...] = ready[N : 2 * N, :]
    held[...] = four[...]
    side = ready[2 * N : 2 * N + 8, :]
    invert(ar, ai)
    mat[0] = ar[...]
    mat[1] = ai[...]
    q_r, q_i = apply((side[0:1], side[1:2]), ar[...], ai[...])
    vec[...] = jnp.concatenate([-q_r, -q_i, side[2:8]], 0)


def last_kernel(flag, weight, far, m0, v0, m1, v1, m4, v4, m7, v7, mid, out, ar, ai):
    side = far[2 * N : 2 * N + 8, :]
    own = v7[...]
    middle = jnp.where(flag[0] == 1, side[3:4], own[3:4])
    scale = down(middle) * middle
    ar[...] = far[0:N, :] + scale * m7[0]
    ai[...] = far[N : 2 * N, :] + scale * m7[1]
    rhs = (side[0:1] + middle * own[0:1], side[1:2] + middle * own[1:2])
    invert(ar, ai)
    v_r, v_i = apply(rhs, ar[...], ai[...])
    psi = {8: (-v_r, -v_i)}
    scaled = lambda c, v: (c * v[0], c * v[1])

    def back(q, link, later, mat_r, mat_i):
        add = apply(scaled(link, later), mat_r, mat_i)
        return q[0:1] - add[0], q[1:2] - add[1]

    psi[7] = back(own, middle, psi[8], m7[0], m7[1])
    four = v4[...]
    c4, c6 = four[3:4], four[4:5]
    t = mid[5 * N : 5 * N + 8, :]
    right = scaled(c6, psi[7])
    w = apply(right, mid[0:N, :], mid[N : 2 * N, :], turned=True)
    psi[4] = back(four, c4, w, m4[0], m4[1])
    left = scaled(c4, psi[4])
    a = apply(left, *unfold(mid[2 * N : 3 * N, :], t[4:5]))
    psi[5] = (t[0:1] + a[0] + w[0], t[1:2] + a[1] + w[1])
    b = apply(left, mid[0:N, :], mid[N : 2 * N, :])
    c = apply(right, *unfold(mid[3 * N : 4 * N, :], t[5:6]))
    psi[6] = (t[2:3] + b[0] + c[0], t[3:4] + b[1] + c[1])
    psi[3] = back(v1[1], four[2:3], psi[4], m1[1, 0], m1[1, 1])
    psi[2] = back(v1[0], v1[1, 2:3, :], psi[3], m1[0, 0], m1[0, 1])
    psi[1] = back(v0[1], v1[0, 2:3, :], psi[2], m0[1, 0], m0[1, 1])
    psi[0] = back(v0[0], v0[1, 2:3, :], psi[1], m0[0, 0], m0[0, 1])
    rows = [weight[0] * (psi[j][0] * psi[j][0] + psi[j][1] * psi[j][1]) for j in range(8)]
    out[...] = jnp.where(
        flag[0] == 1, jnp.concatenate(rows[::-1], 0), jnp.concatenate(rows, 0)
    )


SMEM = pl.BlockSpec(memory_space=pltpu.SMEM)
VMEM = pl.BlockSpec(memory_space=pltpu.VMEM)
PARAMS = pltpu.CompilerParams(vmem_limit_bytes=48 * 2**20)
MATRIX = pltpu.VMEM((N, N), jnp.float32)
SIDE = pltpu.VMEM((8, N), jnp.float32)


def shape(*dims):
    return jax.ShapeDtypeStruct(dims, jnp.float32)


def call(kernel, scalars, arrays, outs, scratch, steps=1):
    return pl.pallas_call(
        kernel,
        out_shape=outs,
        in_specs=[SMEM] * len(scalars) + [VMEM] * len(arrays),
        out_specs=jax.tree.map(lambda _: VMEM, outs),
        scratch_shapes=scratch,
        compiler_params=PARAMS,
        cost_estimate=pl.CostEstimate(
            flops=steps * 8 * N**3, bytes_accessed=steps * 4 * N * N, transcendentals=0
        ),
    )(*scalars, *arrays)


def shards(
    occupancy, onsite, defect_shift, site_order, lateral, coupling, energies, weights, sources
):
    slab = lax.axis_index("slab")
    column = lax.axis_index("energy")
    pot_piece = onsite + occupancy.astype(jnp.float32) * defect_shift
    mine = lax.dynamic_slice(site_order, (column * 16,), (16,))
    at = mine[:, None] == lax.broadcasted_iota(jnp.int32, (16, N), 1)
    spread = jnp.sum(jnp.where(at[None], pot_piece[:, :, None], 0.0), axis=1)
    piece = jnp.concatenate([lateral.reshape(32, N), spread, jnp.zeros((6, N), jnp.float32)], 0)
    got = lax.all_to_all(jnp.broadcast_to(piece[None], (16, 40, N)), "energy", 0, 0)
    flip = slab >= 4
    flag = flip.astype(jnp.int32)[None]
    vecs = jnp.stack([coupling, sources[0, 0], sources[1, 0]])
    vecs = jnp.where(flip, vecs[:, ::-1], vecs).reshape(6, N)
    vecs = jnp.concatenate([vecs, jnp.zeros((2, N), jnp.float32)], 0)
    own = call(prep_kernel, [flag], [got, vecs], shape(PACK, N), [])
    after = lax.ppermute(own, "slab", [(1, 0), (6, 7), (3, 2), (4, 5)])
    inner = ((slab == 2) | (slab == 5)).astype(jnp.int32)[None]
    pair = [shape(2, 2, N, N), shape(2, 8, N)]
    square = [shape(2, N, N), shape(8, N)]
    room = [MATRIX, MATRIX]
    sides = pltpu.VMEM((2, 8, N), jnp.float32)
    m0, v0, mid, kept = call(
        first_kernel,
        [flag, inner, energies],
        [own, after],
        pair + [shape(5 * N + 24, N), shape(PACK, N)],
        room + [SIDE, pltpu.VMEM((2, N, N), jnp.float32), sides],
        2,
    )
    mid = lax.ppermute(mid, "slab", [(2, 0), (5, 7)])
    m1, v1 = call(
        second_kernel, [flag, energies], [kept, m0, v0], pair, room + [SIDE, sides], 2
    )
    m4, v4, ready = call(
        third_kernel,
        [flag, energies],
        [m1, v1, mid],
        square + [shape(PACK, N)],
        room,
    )
    far = lax.ppermute(ready, "slab", [(0, 7), (7, 0)])
    m7, v7, m4 = call(inner_kernel, [], [ready, m4], square + [shape(2, N, N)], room)
    density = call(
        last_kernel,
        [flag, weights],
        [far, m0, v0, m1, v1, m4, v4, m7, v7, mid],
        shape(8, N),
        room,
    )
    parts = density.reshape(4, 2, 16, 16)
    low = jnp.where(slab == 0, parts, 0.0)
    high = jnp.where(slab == 7, parts, 0.0)
    sent = jnp.concatenate([low, high], 0).transpose(0, 2, 1, 3).reshape(128, 2, 16)
    return jnp.sum(lax.all_to_all(sent, ("slab", "energy"), 0, 0), axis=0)


def solution(mesh):
    return jax.shard_map(
        shards,
        mesh=mesh,
        in_specs=(
            P("slab", "energy"),
            P("slab", "energy"),
            P("slab", "energy"),
            P(),
            P("slab", "energy", None),
            P("slab", None),
            P("energy"),
            P("energy"),
            P(None, "energy", "slab", None),
        ),
        out_specs=P("slab", "energy"),
        check_vma=False,
    )
```

```python
import functools
import jax
import jax.numpy as jnp
from jax import lax
from jax.experimental import pallas as pl
from jax.experimental.pallas import tpu as pltpu
from jax.sharding import PartitionSpec as P

BROADENING = 1.2
LATERAL_SCALE = 0.9
HIGHEST = lax.Precision.HIGHEST
PACK = 2 * 256 + 8
N=256
W=32
S8=(8,128)
def row(t,s): return jnp.broadcast_to(t[s:s+1],S8)
def lane_of(t,idx): return jnp.take_along_axis(t,idx,axis=1)
def split3(x):
    h=x.astype(jnp.bfloat16); r=x-h.astype(jnp.float32)
    m=r.astype(jnp.bfloat16); l=(r-m.astype(jnp.float32)).astype(jnp.bfloat16)
    return h,m,l
MIX=True
def times(x,y): return (x[0]*y[0]-x[1]*y[1],x[0]*y[1]+x[1]*y[0])
def less(x,a,b): return (x[0]-(a[0]*b[0]-a[1]*b[1]),x[1]-(a[0]*b[1]+a[1]*b[0]))
def row2(x,j): return (row(x[0],j),row(x[1],j))
def panel(T,place,sub,lane):
    half=place//128; off=place-128*half
    nt=W//8
    Z=[]
    for s in range(nt):
        pick=lambda t: tuple(jnp.where(half==0,T[t][0][c],T[t][1][c]) for c in (0,1))
        idx=[jnp.full(S8,off+8*s+j,jnp.int32) for j in range(8)]
        wide=lambda x: [tuple(lane_of(c,idx[j]) for c in x) for j in range(8)]
        C=wide(pick(s))
        O={t:wide(pick(t)) for t in range(s+1,nt)}
        first=place+8*s
        for h in range(2):
            local=lane-(first-128*h)
            inside=(local>=0)&(local<8)
            minus=jnp.where(local==sub,-1.0,0.0)
            for t in range(s,nt):
                r,i=T[t][h]
                T[t][h]=(jnp.where(inside,minus if t==s else 0.0,r),jnp.where(inside,0.0,i))
        X=[T[s][0],T[s][1]]
        Q=None
        rows=[[],[]]
        p=row2(C[0],0)
        for j in range(8):
            inv=1.0/(p[0]*p[0]+p[1]*p[1])
            c=C[j]
            q=(p[0]*inv,-p[1]*inv)
            Q=q if j==0 else tuple(jnp.where(sub==j,a,b) for a,b in zip(q,Q))
            if j<7:
                e=row2(c,j+1)
                g=times(times(e,e),(p[0],-p[1]))
                n=row2(C[j+1],j+1)
                p=(n[0]-g[0]*inv,n[1]-g[1]*inv)
                low=tuple(jnp.where(sub>j,a,0.0) for a in c)
                scaled=times(c,q)
                for j2 in range(j+1,8):
                    w=row2(scaled,j2)
                    C[j2]=less(C[j2],low,w)
                    for t in range(s+1,min(nt,s+2) if MIX else nt): O[t][j2]=less(O[t][j2],O[t][j],w)
            for h in range(2):
                w=times(row2(X[h],j),q)
                rows[h].append(w)
                if j<7: X[h]=less(X[h],low,w)
        T[s]=X
        z=[times(x,Q) for x in X]
        Z.append(z)
        if s<nt-1:
            for h in range(2):
                x=T[s+1][h]
                for j in range(8): x=less(x,O[s+1][j],rows[h][j])
                T[s+1][h]=x
        if s<nt-2:
            if MIX:
                V=list(z)
                for j in range(7,0,-1):
                    u=times(C[j],Q)
                    u=tuple(jnp.where(sub<j,a,0.0) for a in u)
                    V=[less(v,u,row2(v,j)) for v in V]
                rows=[[row2(v,j) for j in range(8)] for v in V]
            for t in range(s+2,nt):
                for h in range(2):
                    x=T[t][h]
                    for j in range(8): x=less(x,O[t][j],rows[h][j])
                    T[t][h]=x
    for t in range(nt-1):
        for h in range(2):
            local=lane-(place-128*h)
            above=(local>=8*t+8)&(local<W)
            T[t][h]=tuple(jnp.where(above,0.0,x) for x in T[t][h])
            Z[t][h]=tuple(jnp.where(above,0.0,x) for x in Z[t][h])
    return T,Z
PR=((0,0),(0,1),(1,0),(1,1),(0,2),(2,0))
def invert(ar,ai):
    sub=lax.broadcasted_iota(jnp.int32,S8,0); lane=lax.broadcasted_iota(jnp.int32,S8,1)
    @pl.loop(0,N//W)
    def _(k):
        place=pl.multiple_of(k*W,W)
        old=[ar[pl.ds(place,W),:],ai[pl.ds(place,W),:]]
        T=[[tuple(old[c][8*t:8*t+8,128*h:128*h+128] for c in (0,1)) for h in (0,1)] for t in range(W//8)]
        Y,Z=panel(T,place,sub,lane)
        whole=lambda M: [jnp.concatenate([jnp.concatenate([m[0][c],m[1][c]],1) for m in M],0) for c in (0,1)]
        ys=[split3(u) for u in whole(Y)]; zs=[split3(v) for v in whole(Z)]; ns=[-v for v in zs[1]]
        left=jnp.concatenate([ys[0][a] for a,_ in PR]+[ys[1][a] for a,_ in PR],0)
        re=jnp.concatenate([zs[0][b] for _,b in PR]+[ns[b] for _,b in PR],0)
        im=jnp.concatenate([zs[1][b] for _,b in PR]+[zs[0][b] for _,b in PR],0)
        right=jnp.concatenate([re,im],1)
        out=lax.dot_general(left,right,(((0,),(0,)),((),())),preferred_element_type=jnp.float32)
        full=lax.broadcasted_iota(jnp.int32,(1,N),1)-place
        keep=jnp.broadcast_to((full<0)|(full>=W),(N,N))
        ar[pl.ds(place,W),:]=jnp.zeros((W,N),jnp.float32)
        ai[pl.ds(place,W),:]=jnp.zeros((W,N),jnp.float32)
        ar[...]=jnp.where(keep,ar[...],0.0)-out[:,:N]
        ai[...]=jnp.where(keep,ai[...],0.0)-out[:,N:]


def prep_kernel(flag, got, vecs, out):
    turned = flag[0]
    for b in range(2):
        rows = jnp.concatenate([got[e, 16 * b : 16 * b + 16, :] for e in range(16)], 0)
        hop = LATERAL_SCALE * (rows + rows.T)
        pot = got[0, 32 + b : 33 + b, :]
        for e in range(1, 16):
            pot = pot + got[e, 32 + b : 33 + b, :]
        on_diag = lax.broadcasted_iota(jnp.int32, (N, N), 0) == lax.broadcasted_iota(
            jnp.int32, (N, N), 1
        )
        place = jnp.where(turned == 1, 1 - b, b) * N
        out[pl.ds(pl.multiple_of(place, N), N), :] = jnp.where(on_diag, -pot - hop, -hop)
    out[2 * N : 2 * N + 8, :] = vecs[...]


def row_times(vector, matrix, turned=False):
    return lax.dot_general(
        vector,
        matrix,
        (((1,), (1 if turned else 0,)), ((), ())),
        precision=HIGHEST,
        preferred_element_type=jnp.float32,
    )


def apply(v, gr, gi, turned=False):
    if not turned:
        tall = [jnp.broadcast_to(x, (128, N)).T for x in v]
        halves = [[], []]
        for h in range(0, N, 128):
            a, b = gr[:, h : h + 128], gi[:, h : h + 128]
            halves[0].append(jnp.sum(tall[0] * a - tall[1] * b, axis=0, keepdims=True))
            halves[1].append(jnp.sum(tall[0] * b + tall[1] * a, axis=0, keepdims=True))
        return jnp.concatenate(halves[0], 1), jnp.concatenate(halves[1], 1)
    both = jnp.concatenate([v[0], v[1], jnp.zeros((6, N), jnp.float32)], 0)
    a = row_times(both, gr, turned)
    b = row_times(both, gi, turned)
    return a[0:1] - b[1:2], a[1:2] + b[0:1]


def product(a, b, turned=False):
    axis = 0 if turned else 1
    a3 = [split3(a[0]), split3(a[1])]
    b3 = [split3(b[0]), split3(b[1])]
    out_r = out_i = 0.0
    for i, j in PR[::-1]:
        left = jnp.concatenate([a3[0][i], a3[1][i]], axis)
        right = jnp.concatenate(
            [
                jnp.concatenate([b3[0][j], b3[1][j]], 1),
                jnp.concatenate([-b3[1][j], b3[0][j]], 1),
            ],
            0,
        )
        out = lax.dot_general(
            left, right, (((axis,), (0,)), ((), ())), preferred_element_type=jnp.float32
        )
        out_r = out_r + out[:, :N]
        out_i = out_i + out[:, N:]
    return out_r, out_i


def on_diagonal():
    return lax.broadcasted_iota(jnp.int32, (N, N), 0) == lax.broadcasted_iota(
        jnp.int32, (N, N), 1
    )


def down(link):
    tall = jnp.broadcast_to(link, (128, N)).T
    return jnp.concatenate([tall, tall], 1)


def load_block(ar, ai, real, link, energy):
    scale = down(link) * link
    diag = on_diagonal()
    ar[...] = real + scale * ar[...] + jnp.where(diag, energy, 0.0)
    ai[...] = scale * ai[...] + jnp.where(diag, BROADENING, 0.0)


def eliminate(flag, energy, bond, source, real, ar, ai, carry, mats, vecs, slot):
    link = jnp.where(flag[0] == 1, bond, carry[3:4, :])
    load_block(ar, ai, real, link, energy[0])
    rhs = (source[0] + link * carry[0:1, :], source[1] + link * carry[1:2, :])
    invert(ar, ai)
    mats[slot, 0] = ar[...]
    mats[slot, 1] = ai[...]
    q_r, q_i = apply(rhs, ar[...], ai[...])
    now = jnp.concatenate([-q_r, -q_i, link, bond, jnp.zeros((4, N), jnp.float32)], 0)
    carry[...] = now
    vecs[slot] = now


def fold(one, two):
    row_id = lax.broadcasted_iota(jnp.int32, (N, N), 0)
    lane_id = lax.broadcasted_iota(jnp.int32, (N, N), 1)
    diag = jnp.sum(jnp.where(row_id == lane_id, two, 0.0), axis=0, keepdims=True)
    return jnp.where(row_id >= lane_id, one, two), diag


def unfold(both, diag):
    row_id = lax.broadcasted_iota(jnp.int32, (N, N), 0)
    lane_id = lax.broadcasted_iota(jnp.int32, (N, N), 1)
    other = both.T
    one = jnp.where(row_id >= lane_id, both, other)
    two = jnp.where(row_id < lane_id, both, jnp.where(row_id == lane_id, diag, other))
    return one, two


def rows_of(pack, b):
    side = pack[2 * N : 2 * N + 8, :]
    return jnp.concatenate([side[b : b + 1], side[2 + b : 3 + b], side[4 + b : 5 + b]], 0)


def start_kernel(flag, inner, energy, own, mats, vecs, ar, ai, carry):
    ar[...] = jnp.zeros((N, N), jnp.float32)
    ai[...] = jnp.zeros((N, N), jnp.float32)
    carry[...] = jnp.zeros((8, N), jnp.float32)
    is_inner = inner[0] == 1
    real = jnp.where(is_inner, own[N : 2 * N, :], own[0:N, :])
    here = jnp.where(is_inner, rows_of(own, 1), rows_of(own, 0))
    eliminate(flag, energy, here[0:1], (here[1:2], here[2:3]), real, ar, ai, carry, mats, vecs, 0)


def first_kernel(
    flag, inner, energy, own, after, old, before, mats, vecs, mid, kept, ar, ai, carry, side
):
    ar[...] = old[0, 0]
    ai[...] = old[0, 1]
    carry[...] = before[0]
    first = own[2 * N : 2 * N + 8, :]
    second = after[2 * N : 2 * N + 8, :]
    is_inner = inner[0] == 1
    kept[...] = after[...]
    real = jnp.where(is_inner, after[0:N, :], own[N : 2 * N, :])
    side[0, 0:3] = rows_of(own, 1)
    side[1, 0:3] = jnp.where(is_inner, rows_of(after, 0), rows_of(own, 1))
    here = side[1]
    mats[0, 0] = old[0, 0]
    mats[0, 1] = old[0, 1]
    vecs[0] = before[0]
    eliminate(flag, energy, here[0:1], (here[1:2], here[2:3]), real, ar, ai, carry, mats, vecs, 1)

    @pl.when(is_inner)
    def _():
        link = carry[2:3, :]
        n5 = (mats[0, 0], mats[0, 1])
        n6 = (mats[1, 0], mats[1, 1])
        m56 = product((n5[0] * link, n5[1] * link), n6)
        m55 = product((m56[0] * link, m56[1] * link), n5)
        m55 = (-n5[0] - m55[0], -n5[1] - m55[1])
        m66 = (-n6[0], -n6[1])
        folded = [fold(*m55), fold(*m66), fold(own[0:N, :], after[N : 2 * N, :])]
        mid[0:N, :] = m56[0]
        mid[N : 2 * N, :] = m56[1]
        for i in range(3):
            mid[(2 + i) * N : (3 + i) * N, :] = folded[i][0]
        s5 = (side[0, 1:2, :], side[0, 2:3, :])
        s6 = (side[1, 1:2, :], side[1, 2:3, :])
        a = apply(s5, *m55)
        b = apply(s6, *m56, turned=True)
        c = apply(s5, *m56)
        d = apply(s6, *m66)
        zero = jnp.zeros((1, N), jnp.float32)
        mid[5 * N : 5 * N + 8, :] = jnp.concatenate(
            [a[0] + b[0], a[1] + b[1], c[0] + d[0], c[1] + d[1]]
            + [folded[i][1] for i in range(3)]
            + [zero],
            0,
        )
        mid[5 * N + 8 : 5 * N + 16, :] = first
        mid[5 * N + 16 : 5 * N + 24, :] = second


def second_kernel(flag, energy, after, start, before, mats, vecs, ar, ai, carry, side):
    ar[...] = start[1, 0]
    ai[...] = start[1, 1]
    carry[...] = before[1]
    have = after[2 * N : 2 * N + 8, :]
    for b in range(2):
        side[b, 0:3] = jnp.concatenate(
            [have[b : b + 1], have[2 + b : 3 + b], have[4 + b : 5 + b]], 0
        )

    @pl.loop(0, 2)
    def _(b):
        here = side[b]
        real = after[pl.ds(pl.multiple_of(b * N, N), N), :]
        eliminate(
            flag, energy, here[0:1], (here[1:2], here[2:3]), real, ar, ai, carry, mats, vecs, b
        )


def third_kernel(flag, energy, start, before, mid, mat, vec, ready, ar, ai):
    p2 = mid[5 * N + 8 : 5 * N + 16, :]
    p3 = mid[5 * N + 16 : 5 * N + 24, :]
    back = flag[0] == 1
    link = jnp.where(back, p2[0:1], before[1, 3:4, :])
    c4 = jnp.where(back, p2[1:2], p2[0:1])
    c6 = jnp.where(back, p3[1:2], p3[0:1])
    t = mid[5 * N : 5 * N + 8, :]
    ar[...] = start[1, 0]
    ai[...] = start[1, 1]
    a4, a7 = unfold(mid[4 * N : 5 * N, :], t[6:7])
    m55 = unfold(mid[2 * N : 3 * N, :], t[4:5])
    m66 = unfold(mid[3 * N : 4 * N, :], t[5:6])
    load_block(ar, ai, a4, link, energy[0])
    down4 = down(c4)
    square = down4 * c4
    ar[...] = ar[...] - square * m55[0]
    ai[...] = ai[...] - square * m55[1]
    rhs = (
        p2[2:3] + link * before[1, 0:1, :] + c4 * t[0:1],
        p2[4:5] + link * before[1, 1:2, :] + c4 * t[1:2],
    )
    invert(ar, ai)
    mat[0] = ar[...]
    mat[1] = ai[...]
    n_r, n_i = apply(rhs, ar[...], ai[...])
    q = (-n_r, -n_i)
    vec[...] = jnp.concatenate([q[0], q[1], link, c4, c6, jnp.zeros((3, N), jnp.float32)], 0)
    cross = down4 * c6
    ready[0:N, :] = cross * mid[0:N, :]
    ready[N : 2 * N, :] = cross * mid[N : 2 * N, :]
    k = (ready[0:N, :], ready[N : 2 * N, :])
    x = product((ar[...], ai[...]), k)
    y = product(k, x, turned=True)
    onto = apply(q, *k)
    square = down(c6) * c6
    diag = on_diagonal()
    ready[0:N, :] = (
        a7 + jnp.where(diag, energy[0], 0.0) - square * m66[0] + y[0]
    )
    ready[N : 2 * N, :] = (
        jnp.where(diag, BROADENING, 0.0) - square * m66[1] + y[1]
    )
    ready[2 * N : 2 * N + 8, :] = jnp.concatenate(
        [
            p3[3:4] + c6 * t[2:3] + onto[0],
            p3[5:6] + c6 * t[3:4] + onto[1],
            link,
            p3[1:2],
            jnp.zeros((4, N), jnp.float32),
        ],
        0,
    )


def inner_kernel(ready, four, mat, vec, held, ar, ai):
    ar[...] = ready[0:N, :]
    ai[...] = ready[N : 2 * N, :]
    held[...] = four[...]
    side = ready[2 * N : 2 * N + 8, :]
    invert(ar, ai)
    mat[0] = ar[...]
    mat[1] = ai[...]
    q_r, q_i = apply((side[0:1], side[1:2]), ar[...], ai[...])
    vec[...] = jnp.concatenate([-q_r, -q_i, side[2:8]], 0)


def last_kernel(flag, weight, far, m0, v0, m1, v1, m4, v4, m7, v7, mid, out, ar, ai):
    side = far[2 * N : 2 * N + 8, :]
    own = v7[...]
    middle = jnp.where(flag[0] == 1, side[3:4], own[3:4])
    scale = down(middle) * middle
    ar[...] = far[0:N, :] + scale * m7[0]
    ai[...] = far[N : 2 * N, :] + scale * m7[1]
    rhs = (side[0:1] + middle * own[0:1], side[1:2] + middle * own[1:2])
    invert(ar, ai)
    v_r, v_i = apply(rhs, ar[...], ai[...])
    psi = {8: (-v_r, -v_i)}
    scaled = lambda c, v: (c * v[0], c * v[1])

    def back(q, link, later, mat_r, mat_i):
        add = apply(scaled(link, later), mat_r, mat_i)
        return q[0:1] - add[0], q[1:2] - add[1]

    psi[7] = back(own, middle, psi[8], m7[0], m7[1])
    four = v4[...]
    c4, c6 = four[3:4], four[4:5]
    t = mid[5 * N : 5 * N + 8, :]
    right = scaled(c6, psi[7])
    w = apply(right, mid[0:N, :], mid[N : 2 * N, :], turned=True)
    psi[4] = back(four, c4, w, m4[0], m4[1])
    left = scaled(c4, psi[4])
    a = apply(left, *unfold(mid[2 * N : 3 * N, :], t[4:5]))
    psi[5] = (t[0:1] + a[0] + w[0], t[1:2] + a[1] + w[1])
    b = apply(left, mid[0:N, :], mid[N : 2 * N, :])
    c = apply(right, *unfold(mid[3 * N : 4 * N, :], t[5:6]))
    psi[6] = (t[2:3] + b[0] + c[0], t[3:4] + b[1] + c[1])
    psi[3] = back(v1[1], four[2:3], psi[4], m1[1, 0], m1[1, 1])
    psi[2] = back(v1[0], v1[1, 2:3, :], psi[3], m1[0, 0], m1[0, 1])
    psi[1] = back(v0[1], v1[0, 2:3, :], psi[2], m0[1, 0], m0[1, 1])
    psi[0] = back(v0[0], v0[1, 2:3, :], psi[1], m0[0, 0], m0[0, 1])
    rows = [weight[0] * (psi[j][0] * psi[j][0] + psi[j][1] * psi[j][1]) for j in range(8)]
    out[...] = jnp.where(
        flag[0] == 1, jnp.concatenate(rows[::-1], 0), jnp.concatenate(rows, 0)
    )


SMEM = pl.BlockSpec(memory_space=pltpu.SMEM)
VMEM = pl.BlockSpec(memory_space=pltpu.VMEM)
PARAMS = pltpu.CompilerParams(vmem_limit_bytes=16 * 2**20)
MATRIX = pltpu.VMEM((N, N), jnp.float32)
SIDE = pltpu.VMEM((8, N), jnp.float32)


def shape(*dims):
    return jax.ShapeDtypeStruct(dims, jnp.float32)


def call(kernel, scalars, arrays, outs, scratch, steps=1):
    return pl.pallas_call(
        kernel,
        out_shape=outs,
        in_specs=[SMEM] * len(scalars) + [VMEM] * len(arrays),
        out_specs=jax.tree.map(lambda _: VMEM, outs),
        scratch_shapes=scratch,
        compiler_params=PARAMS,
        cost_estimate=pl.CostEstimate(
            flops=steps * 8 * N**3, bytes_accessed=steps * 4 * N * N, transcendentals=0
        ),
    )(*scalars, *arrays)


def shards(
    occupancy, onsite, defect_shift, site_order, lateral, coupling, energies, weights, sources
):
    slab = lax.axis_index("slab")
    column = lax.axis_index("energy")
    pot_piece = onsite + occupancy.astype(jnp.float32) * defect_shift
    mine = lax.dynamic_slice(site_order, (column * 16,), (16,))
    at = mine[:, None] == lax.broadcasted_iota(jnp.int32, (16, N), 1)
    spread = jnp.sum(jnp.where(at[None], pot_piece[:, :, None], 0.0), axis=1)
    piece = jnp.concatenate([lateral.reshape(32, N), spread, jnp.zeros((6, N), jnp.float32)], 0)
    got = lax.all_to_all(jnp.broadcast_to(piece[None], (16, 40, N)), "energy", 0, 0)
    flip = slab >= 4
    flag = flip.astype(jnp.int32)[None]
    vecs = jnp.stack([coupling, sources[0, 0], sources[1, 0]])
    vecs = jnp.where(flip, vecs[:, ::-1], vecs).reshape(6, N)
    vecs = jnp.concatenate([vecs, jnp.zeros((2, N), jnp.float32)], 0)
    own = call(prep_kernel, [flag], [got, vecs], shape(PACK, N), [])
    after = lax.ppermute(own, "slab", [(1, 0), (6, 7), (3, 2), (4, 5)])
    inner = ((slab == 2) | (slab == 5)).astype(jnp.int32)[None]
    pair = [shape(2, 2, N, N), shape(2, 8, N)]
    square = [shape(2, N, N), shape(8, N)]
    room = [MATRIX, MATRIX]
    sides = pltpu.VMEM((2, 8, N), jnp.float32)
    old, before = call(
        start_kernel,
        [flag, inner, energies],
        [own],
        [shape(1, 2, N, N), shape(1, 8, N)],
        room + [SIDE],
    )
    m0, v0, mid, kept = call(
        first_kernel,
        [flag, inner, energies],
        [own, after, old, before],
        pair + [shape(5 * N + 24, N), shape(PACK, N)],
        room + [SIDE, sides],
    )
    mid = lax.ppermute(mid, "slab", [(2, 0), (5, 7)])
    m1, v1 = call(
        second_kernel, [flag, energies], [kept, m0, v0], pair, room + [SIDE, sides], 2
    )
    m4, v4, ready = call(
        third_kernel,
        [flag, energies],
        [m1, v1, mid],
        square + [shape(PACK, N)],
        room,
    )
    far = lax.ppermute(ready, "slab", [(0, 7), (7, 0)])
    m7, v7, m4 = call(inner_kernel, [], [ready, m4], square + [shape(2, N, N)], room)
    density = call(
        last_kernel,
        [flag, weights],
        [far, m0, v0, m1, v1, m4, v4, m7, v7, mid],
        shape(8, N),
        room,
    )
    parts = density.reshape(4, 2, 16, 16)
    low = jnp.where(slab == 0, parts, 0.0)
    high = jnp.where(slab == 7, parts, 0.0)
    sent = jnp.concatenate([low, high], 0).transpose(0, 2, 1, 3).reshape(128, 2, 16)
    return jnp.sum(lax.all_to_all(sent, ("slab", "energy"), 0, 0), axis=0)


def solution(mesh):
    return jax.shard_map(
        shards,
        mesh=mesh,
        in_specs=(
            P("slab", "energy"),
            P("slab", "energy"),
            P("slab", "energy"),
            P(),
            P("slab", "energy", None),
            P("slab", None),
            P("energy"),
            P("energy"),
            P(None, "energy", "slab", None),
        ),
        out_specs=P("slab", "energy"),
        check_vma=False,
    )
```

```python
import functools
import jax
import jax.numpy as jnp
from jax import lax
from jax.experimental import pallas as pl
from jax.experimental.pallas import tpu as pltpu
from jax.sharding import PartitionSpec as P

BROADENING = 1.2
LATERAL_SCALE = 0.9
HIGHEST = lax.Precision.HIGHEST
PACK = 2 * 256 + 8
N=256
W=32
S8=(8,128)
def row(t,s): return jnp.broadcast_to(t[s:s+1],S8)
def lane_of(t,idx): return jnp.take_along_axis(t,idx,axis=1)
def split3(x):
    h=x.astype(jnp.bfloat16); r=x-h.astype(jnp.float32)
    m=r.astype(jnp.bfloat16); l=(r-m.astype(jnp.float32)).astype(jnp.bfloat16)
    return h,m,l
MIX=True
def times(x,y): return (x[0]*y[0]-x[1]*y[1],x[0]*y[1]+x[1]*y[0])
def less(x,a,b): return (x[0]-(a[0]*b[0]-a[1]*b[1]),x[1]-(a[0]*b[1]+a[1]*b[0]))
def row2(x,j): return (row(x[0],j),row(x[1],j))
def panel(T,place,half,sub,lane):
    off=place-128*half
    nt=W//8
    Z=[]
    for s in range(nt):
        pick=lambda t: T[t][half]
        idx=[jnp.full(S8,off+8*s+j,jnp.int32) for j in range(8)]
        wide=lambda x: [tuple(lane_of(c,idx[j]) for c in x) for j in range(8)]
        C=wide(pick(s))
        O={t:wide(pick(t)) for t in range(s+1,nt)}
        first=place+8*s
        for h in (half,):
            local=lane-(first-128*h)
            inside=(local>=0)&(local<8)
            minus=jnp.where(local==sub,-1.0,0.0)
            for t in range(s,nt):
                r,i=T[t][h]
                T[t][h]=(jnp.where(inside,minus if t==s else 0.0,r),jnp.where(inside,0.0,i))
        X=[T[s][0],T[s][1]]
        Q=None
        rows=[[],[]]
        p=row2(C[0],0)
        for j in range(8):
            inv=1.0/(p[0]*p[0]+p[1]*p[1])
            c=C[j]
            q=(p[0]*inv,-p[1]*inv)
            Q=q if j==0 else tuple(jnp.where(sub==j,a,b) for a,b in zip(q,Q))
            if j<7:
                e=row2(c,j+1)
                g=times(times(e,e),(p[0],-p[1]))
                n=row2(C[j+1],j+1)
                p=(n[0]-g[0]*inv,n[1]-g[1]*inv)
                low=tuple(jnp.where(sub>j,a,0.0) for a in c)
                scaled=times(c,q)
                for j2 in range(j+1,8):
                    w=row2(scaled,j2)
                    C[j2]=less(C[j2],low,w)
                    for t in range(s+1,min(nt,s+2) if MIX else nt): O[t][j2]=less(O[t][j2],O[t][j],w)
            for h in range(2):
                w=times(row2(X[h],j),q)
                rows[h].append(w)
                if j<7: X[h]=less(X[h],low,w)
        T[s]=X
        z=[times(x,Q) for x in X]
        Z.append(z)
        if s<nt-1:
            for h in range(2):
                x=T[s+1][h]
                for j in range(8): x=less(x,O[s+1][j],rows[h][j])
                T[s+1][h]=x
        if s<nt-2:
            if MIX:
                V=list(z)
                for j in range(7,0,-1):
                    u=times(C[j],Q)
                    u=tuple(jnp.where(sub<j,a,0.0) for a in u)
                    V=[less(v,u,row2(v,j)) for v in V]
                rows=[[row2(v,j) for j in range(8)] for v in V]
            for t in range(s+2,nt):
                for h in range(2):
                    x=T[t][h]
                    for j in range(8): x=less(x,O[t][j],rows[h][j])
                    T[t][h]=x
    for t in range(nt-1):
        for h in (half,):
            local=lane-(place-128*h)
            above=(local>=8*t+8)&(local<W)
            T[t][h]=tuple(jnp.where(above,0.0,x) for x in T[t][h])
            Z[t][h]=tuple(jnp.where(above,0.0,x) for x in Z[t][h])
    return T,Z
PR=((0,0),(0,1),(1,0),(1,1),(0,2),(2,0))
def invert(ar,ai):
    sub=lax.broadcasted_iota(jnp.int32,S8,0); lane=lax.broadcasted_iota(jnp.int32,S8,1)
    for half in (0,1):
      @pl.loop(0,128//W)
      def _(k):
        place=pl.multiple_of(k*W+128*half,W)
        old=[ar[pl.ds(place,W),:],ai[pl.ds(place,W),:]]
        T=[[tuple(old[c][8*t:8*t+8,128*h:128*h+128] for c in (0,1)) for h in (0,1)] for t in range(W//8)]
        Y,Z=panel(T,place,half,sub,lane)
        whole=lambda M: [jnp.concatenate([jnp.concatenate([m[0][c],m[1][c]],1) for m in M],0) for c in (0,1)]
        ys=[split3(u) for u in whole(Y)]; zs=[split3(v) for v in whole(Z)]; ns=[-v for v in zs[1]]
        left=jnp.concatenate([ys[0][a] for a,_ in PR]+[ys[1][a] for a,_ in PR],0)
        re=jnp.concatenate([zs[0][b] for _,b in PR]+[ns[b] for _,b in PR],0)
        im=jnp.concatenate([zs[1][b] for _,b in PR]+[zs[0][b] for _,b in PR],0)
        right=jnp.concatenate([re,im],1)
        out=lax.dot_general(left,right,(((0,),(0,)),((),())),preferred_element_type=jnp.float32)
        spot=place-128*half
        full=lax.broadcasted_iota(jnp.int32,(1,128),1)
        keep=jnp.broadcast_to((full<spot)|(full>=spot+W),(N,128))
        for ref,at in ((ar,0),(ai,N)):
            ref[pl.ds(place,W),:]=jnp.zeros((W,N),jnp.float32)
            for h in (0,1):
                lanes=slice(128*h,128*h+128)
                was=ref[:,lanes]
                if h==half: was=jnp.where(keep,was,0.0)
                ref[:,lanes]=was-out[:,at+128*h:at+128*h+128]


def prep_kernel(flag, got, vecs, out):
    turned = flag[0]
    for b in range(2):
        rows = jnp.concatenate([got[e, 16 * b : 16 * b + 16, :] for e in range(16)], 0)
        hop = LATERAL_SCALE * (rows + rows.T)
        pot = got[0, 32 + b : 33 + b, :]
        for e in range(1, 16):
            pot = pot + got[e, 32 + b : 33 + b, :]
        on_diag = lax.broadcasted_iota(jnp.int32, (N, N), 0) == lax.broadcasted_iota(
            jnp.int32, (N, N), 1
        )
        place = jnp.where(turned == 1, 1 - b, b) * N
        out[pl.ds(pl.multiple_of(place, N), N), :] = jnp.where(on_diag, -pot - hop, -hop)
    out[2 * N : 2 * N + 8, :] = vecs[...]


def row_times(vector, matrix, turned=False):
    return lax.dot_general(
        vector,
        matrix,
        (((1,), (1 if turned else 0,)), ((), ())),
        precision=HIGHEST,
        preferred_element_type=jnp.float32,
    )


def apply(v, gr, gi, turned=False):
    if not turned:
        tall = [jnp.broadcast_to(x, (128, N)).T for x in v]
        halves = [[], []]
        for h in range(0, N, 128):
            a, b = gr[:, h : h + 128], gi[:, h : h + 128]
            halves[0].append(jnp.sum(tall[0] * a - tall[1] * b, axis=0, keepdims=True))
            halves[1].append(jnp.sum(tall[0] * b + tall[1] * a, axis=0, keepdims=True))
        return jnp.concatenate(halves[0], 1), jnp.concatenate(halves[1], 1)
    both = jnp.concatenate([v[0], v[1], jnp.zeros((6, N), jnp.float32)], 0)
    a = row_times(both, gr, turned)
    b = row_times(both, gi, turned)
    return a[0:1] - b[1:2], a[1:2] + b[0:1]


def product(a, b, turned=False):
    axis = 0 if turned else 1
    a3 = [split3(a[0]), split3(a[1])]
    b3 = [split3(b[0]), split3(b[1])]
    out_r = out_i = 0.0
    for i, j in PR[::-1]:
        left = jnp.concatenate([a3[0][i], a3[1][i]], axis)
        right = jnp.concatenate(
            [
                jnp.concatenate([b3[0][j], b3[1][j]], 1),
                jnp.concatenate([-b3[1][j], b3[0][j]], 1),
            ],
            0,
        )
        out = lax.dot_general(
            left, right, (((axis,), (0,)), ((), ())), preferred_element_type=jnp.float32
        )
        out_r = out_r + out[:, :N]
        out_i = out_i + out[:, N:]
    return out_r, out_i


def on_diagonal():
    return lax.broadcasted_iota(jnp.int32, (N, N), 0) == lax.broadcasted_iota(
        jnp.int32, (N, N), 1
    )


def down(link):
    tall = jnp.broadcast_to(link, (128, N)).T
    return jnp.concatenate([tall, tall], 1)


def load_block(ar, ai, real, link, energy):
    scale = down(link) * link
    diag = on_diagonal()
    ar[...] = real + scale * ar[...] + jnp.where(diag, energy, 0.0)
    ai[...] = scale * ai[...] + jnp.where(diag, BROADENING, 0.0)


def eliminate(flag, energy, bond, source, real, ar, ai, carry, mats, vecs, slot):
    link = jnp.where(flag[0] == 1, bond, carry[3:4, :])
    load_block(ar, ai, real, link, energy[0])
    rhs = (source[0] + link * carry[0:1, :], source[1] + link * carry[1:2, :])
    invert(ar, ai)
    mats[slot, 0] = ar[...]
    mats[slot, 1] = ai[...]
    q_r, q_i = apply(rhs, ar[...], ai[...])
    now = jnp.concatenate([-q_r, -q_i, link, bond, jnp.zeros((4, N), jnp.float32)], 0)
    carry[...] = now
    vecs[slot] = now


def fold(one, two):
    row_id = lax.broadcasted_iota(jnp.int32, (N, N), 0)
    lane_id = lax.broadcasted_iota(jnp.int32, (N, N), 1)
    diag = jnp.sum(jnp.where(row_id == lane_id, two, 0.0), axis=0, keepdims=True)
    return jnp.where(row_id >= lane_id, one, two), diag


def unfold(both, diag):
    row_id = lax.broadcasted_iota(jnp.int32, (N, N), 0)
    lane_id = lax.broadcasted_iota(jnp.int32, (N, N), 1)
    other = both.T
    one = jnp.where(row_id >= lane_id, both, other)
    two = jnp.where(row_id < lane_id, both, jnp.where(row_id == lane_id, diag, other))
    return one, two


def rows_of(pack, b):
    side = pack[2 * N : 2 * N + 8, :]
    return jnp.concatenate([side[b : b + 1], side[2 + b : 3 + b], side[4 + b : 5 + b]], 0)


def start_kernel(flag, inner, energy, own, mats, vecs, ar, ai, carry):
    ar[...] = jnp.zeros((N, N), jnp.float32)
    ai[...] = jnp.zeros((N, N), jnp.float32)
    carry[...] = jnp.zeros((8, N), jnp.float32)
    is_inner = inner[0] == 1
    real = jnp.where(is_inner, own[N : 2 * N, :], own[0:N, :])
    here = jnp.where(is_inner, rows_of(own, 1), rows_of(own, 0))
    eliminate(flag, energy, here[0:1], (here[1:2], here[2:3]), real, ar, ai, carry, mats, vecs, 0)


def first_kernel(
    flag, inner, energy, own, after, old, before, mats, vecs, mid, kept, ar, ai, carry, side
):
    ar[...] = old[0, 0]
    ai[...] = old[0, 1]
    carry[...] = before[0]
    first = own[2 * N : 2 * N + 8, :]
    second = after[2 * N : 2 * N + 8, :]
    is_inner = inner[0] == 1
    kept[...] = after[...]
    real = jnp.where(is_inner, after[0:N, :], own[N : 2 * N, :])
    side[0, 0:3] = rows_of(own, 1)
    side[1, 0:3] = jnp.where(is_inner, rows_of(after, 0), rows_of(own, 1))
    here = side[1]
    mats[0, 0] = old[0, 0]
    mats[0, 1] = old[0, 1]
    vecs[0] = before[0]
    eliminate(flag, energy, here[0:1], (here[1:2], here[2:3]), real, ar, ai, carry, mats, vecs, 1)

    @pl.when(is_inner)
    def _():
        link = carry[2:3, :]
        n5 = (mats[0, 0], mats[0, 1])
        n6 = (mats[1, 0], mats[1, 1])
        m56 = product((n5[0] * link, n5[1] * link), n6)
        m55 = product((m56[0] * link, m56[1] * link), n5)
        m55 = (-n5[0] - m55[0], -n5[1] - m55[1])
        m66 = (-n6[0], -n6[1])
        folded = [fold(*m55), fold(*m66), fold(own[0:N, :], after[N : 2 * N, :])]
        mid[0:N, :] = m56[0]
        mid[N : 2 * N, :] = m56[1]
        for i in range(3):
            mid[(2 + i) * N : (3 + i) * N, :] = folded[i][0]
        s5 = (side[0, 1:2, :], side[0, 2:3, :])
        s6 = (side[1, 1:2, :], side[1, 2:3, :])
        a = apply(s5, *m55)
        b = apply(s6, *m56, turned=True)
        c = apply(s5, *m56)
        d = apply(s6, *m66)
        zero = jnp.zeros((1, N), jnp.float32)
        mid[5 * N : 5 * N + 8, :] = jnp.concatenate(
            [a[0] + b[0], a[1] + b[1], c[0] + d[0], c[1] + d[1]]
            + [folded[i][1] for i in range(3)]
            + [zero],
            0,
        )
        mid[5 * N + 8 : 5 * N + 16, :] = first
        mid[5 * N + 16 : 5 * N + 24, :] = second


def second_kernel(flag, energy, after, start, before, mats, vecs, ar, ai, carry, side):
    ar[...] = start[1, 0]
    ai[...] = start[1, 1]
    carry[...] = before[1]
    have = after[2 * N : 2 * N + 8, :]
    for b in range(2):
        side[b, 0:3] = jnp.concatenate(
            [have[b : b + 1], have[2 + b : 3 + b], have[4 + b : 5 + b]], 0
        )

    @pl.loop(0, 2)
    def _(b):
        here = side[b]
        real = after[pl.ds(pl.multiple_of(b * N, N), N), :]
        eliminate(
            flag, energy, here[0:1], (here[1:2], here[2:3]), real, ar, ai, carry, mats, vecs, b
        )


def third_kernel(flag, energy, start, before, mid, mat, vec, ready, ar, ai):
    p2 = mid[5 * N + 8 : 5 * N + 16, :]
    p3 = mid[5 * N + 16 : 5 * N + 24, :]
    back = flag[0] == 1
    link = jnp.where(back, p2[0:1], before[1, 3:4, :])
    c4 = jnp.where(back, p2[1:2], p2[0:1])
    c6 = jnp.where(back, p3[1:2], p3[0:1])
    t = mid[5 * N : 5 * N + 8, :]
    ar[...] = start[1, 0]
    ai[...] = start[1, 1]
    a4, a7 = unfold(mid[4 * N : 5 * N, :], t[6:7])
    m55 = unfold(mid[2 * N : 3 * N, :], t[4:5])
    m66 = unfold(mid[3 * N : 4 * N, :], t[5:6])
    load_block(ar, ai, a4, link, energy[0])
    down4 = down(c4)
    square = down4 * c4
    ar[...] = ar[...] - square * m55[0]
    ai[...] = ai[...] - square * m55[1]
    rhs = (
        p2[2:3] + link * before[1, 0:1, :] + c4 * t[0:1],
        p2[4:5] + link * before[1, 1:2, :] + c4 * t[1:2],
    )
    invert(ar, ai)
    mat[0] = ar[...]
    mat[1] = ai[...]
    n_r, n_i = apply(rhs, ar[...], ai[...])
    q = (-n_r, -n_i)
    vec[...] = jnp.concatenate([q[0], q[1], link, c4, c6, jnp.zeros((3, N), jnp.float32)], 0)
    cross = down4 * c6
    ready[0:N, :] = cross * mid[0:N, :]
    ready[N : 2 * N, :] = cross * mid[N : 2 * N, :]
    k = (ready[0:N, :], ready[N : 2 * N, :])
    x = product((ar[...], ai[...]), k)
    y = product(k, x, turned=True)
    onto = apply(q, *k)
    square = down(c6) * c6
    diag = on_diagonal()
    ready[0:N, :] = (
        a7 + jnp.where(diag, energy[0], 0.0) - square * m66[0] + y[0]
    )
    ready[N : 2 * N, :] = (
        jnp.where(diag, BROADENING, 0.0) - square * m66[1] + y[1]
    )
    ready[2 * N : 2 * N + 8, :] = jnp.concatenate(
        [
            p3[3:4] + c6 * t[2:3] + onto[0],
            p3[5:6] + c6 * t[3:4] + onto[1],
            link,
            p3[1:2],
            jnp.zeros((4, N), jnp.float32),
        ],
        0,
    )


def inner_kernel(ready, four, mat, vec, held, ar, ai):
    ar[...] = ready[0:N, :]
    ai[...] = ready[N : 2 * N, :]
    held[...] = four[...]
    side = ready[2 * N : 2 * N + 8, :]
    invert(ar, ai)
    mat[0] = ar[...]
    mat[1] = ai[...]
    q_r, q_i = apply((side[0:1], side[1:2]), ar[...], ai[...])
    vec[...] = jnp.concatenate([-q_r, -q_i, side[2:8]], 0)


def last_kernel(flag, weight, far, m0, v0, m1, v1, m4, v4, m7, v7, mid, out, ar, ai):
    side = far[2 * N : 2 * N + 8, :]
    own = v7[...]
    middle = jnp.where(flag[0] == 1, side[3:4], own[3:4])
    scale = down(middle) * middle
    ar[...] = far[0:N, :] + scale * m7[0]
    ai[...] = far[N : 2 * N, :] + scale * m7[1]
    rhs = (side[0:1] + middle * own[0:1], side[1:2] + middle * own[1:2])
    invert(ar, ai)
    v_r, v_i = apply(rhs, ar[...], ai[...])
    psi = {8: (-v_r, -v_i)}
    scaled = lambda c, v: (c * v[0], c * v[1])

    def back(q, link, later, mat_r, mat_i):
        add = apply(scaled(link, later), mat_r, mat_i)
        return q[0:1] - add[0], q[1:2] - add[1]

    psi[7] = back(own, middle, psi[8], m7[0], m7[1])
    four = v4[...]
    c4, c6 = four[3:4], four[4:5]
    t = mid[5 * N : 5 * N + 8, :]
    right = scaled(c6, psi[7])
    w = apply(right, mid[0:N, :], mid[N : 2 * N, :], turned=True)
    psi[4] = back(four, c4, w, m4[0], m4[1])
    left = scaled(c4, psi[4])
    a = apply(left, *unfold(mid[2 * N : 3 * N, :], t[4:5]))
    psi[5] = (t[0:1] + a[0] + w[0], t[1:2] + a[1] + w[1])
    b = apply(left, mid[0:N, :], mid[N : 2 * N, :])
    c = apply(right, *unfold(mid[3 * N : 4 * N, :], t[5:6]))
    psi[6] = (t[2:3] + b[0] + c[0], t[3:4] + b[1] + c[1])
    psi[3] = back(v1[1], four[2:3], psi[4], m1[1, 0], m1[1, 1])
    psi[2] = back(v1[0], v1[1, 2:3, :], psi[3], m1[0, 0], m1[0, 1])
    psi[1] = back(v0[1], v1[0, 2:3, :], psi[2], m0[1, 0], m0[1, 1])
    psi[0] = back(v0[0], v0[1, 2:3, :], psi[1], m0[0, 0], m0[0, 1])
    rows = [weight[0] * (psi[j][0] * psi[j][0] + psi[j][1] * psi[j][1]) for j in range(8)]
    out[...] = jnp.where(
        flag[0] == 1, jnp.concatenate(rows[::-1], 0), jnp.concatenate(rows, 0)
    )


SMEM = pl.BlockSpec(memory_space=pltpu.SMEM)
VMEM = pl.BlockSpec(memory_space=pltpu.VMEM)
PARAMS = pltpu.CompilerParams(vmem_limit_bytes=16 * 2**20)
MATRIX = pltpu.VMEM((N, N), jnp.float32)
SIDE = pltpu.VMEM((8, N), jnp.float32)


def shape(*dims):
    return jax.ShapeDtypeStruct(dims, jnp.float32)


def call(kernel, scalars, arrays, outs, scratch, steps=1):
    return pl.pallas_call(
        kernel,
        out_shape=outs,
        in_specs=[SMEM] * len(scalars) + [VMEM] * len(arrays),
        out_specs=jax.tree.map(lambda _: VMEM, outs),
        scratch_shapes=scratch,
        compiler_params=PARAMS,
        cost_estimate=pl.CostEstimate(
            flops=steps * 8 * N**3, bytes_accessed=steps * 4 * N * N, transcendentals=0
        ),
    )(*scalars, *arrays)


def shards(
    occupancy, onsite, defect_shift, site_order, lateral, coupling, energies, weights, sources
):
    slab = lax.axis_index("slab")
    column = lax.axis_index("energy")
    pot_piece = onsite + occupancy.astype(jnp.float32) * defect_shift
    mine = lax.dynamic_slice(site_order, (column * 16,), (16,))
    at = mine[:, None] == lax.broadcasted_iota(jnp.int32, (16, N), 1)
    spread = jnp.sum(jnp.where(at[None], pot_piece[:, :, None], 0.0), axis=1)
    piece = jnp.concatenate([lateral.reshape(32, N), spread, jnp.zeros((6, N), jnp.float32)], 0)
    got = lax.all_to_all(jnp.broadcast_to(piece[None], (16, 40, N)), "energy", 0, 0)
    flip = slab >= 4
    flag = flip.astype(jnp.int32)[None]
    vecs = jnp.stack([coupling, sources[0, 0], sources[1, 0]])
    vecs = jnp.where(flip, vecs[:, ::-1], vecs).reshape(6, N)
    vecs = jnp.concatenate([vecs, jnp.zeros((2, N), jnp.float32)], 0)
    own = call(prep_kernel, [flag], [got, vecs], shape(PACK, N), [])
    after = lax.ppermute(own, "slab", [(1, 0), (6, 7), (3, 2), (4, 5)])
    inner = ((slab == 2) | (slab == 5)).astype(jnp.int32)[None]
    pair = [shape(2, 2, N, N), shape(2, 8, N)]
    square = [shape(2, N, N), shape(8, N)]
    room = [MATRIX, MATRIX]
    sides = pltpu.VMEM((2, 8, N), jnp.float32)
    old, before = call(
        start_kernel,
        [flag, inner, energies],
        [own],
        [shape(1, 2, N, N), shape(1, 8, N)],
        room + [SIDE],
    )
    m0, v0, mid, kept = call(
        first_kernel,
        [flag, inner, energies],
        [own, after, old, before],
        pair + [shape(5 * N + 24, N), shape(PACK, N)],
        room + [SIDE, sides],
    )
    mid = lax.ppermute(mid, "slab", [(2, 0), (5, 7)])
    m1, v1 = call(
        second_kernel, [flag, energies], [kept, m0, v0], pair, room + [SIDE, sides], 2
    )
    m4, v4, ready = call(
        third_kernel,
        [flag, energies],
        [m1, v1, mid],
        square + [shape(PACK, N)],
        room,
    )
    far = lax.ppermute(ready, "slab", [(0, 7), (7, 0)])
    m7, v7, m4 = call(inner_kernel, [], [ready, m4], square + [shape(2, N, N)], room)
    density = call(
        last_kernel,
        [flag, weights],
        [far, m0, v0, m1, v1, m4, v4, m7, v7, mid],
        shape(8, N),
        room,
    )
    parts = density.reshape(4, 2, 16, 16)
    low = jnp.where(slab == 0, parts, 0.0)
    high = jnp.where(slab == 7, parts, 0.0)
    sent = jnp.concatenate([low, high], 0).transpose(0, 2, 1, 3).reshape(128, 1, 32)
    return jnp.sum(lax.all_to_all(sent, ("slab", "energy"), 0, 0), axis=0).reshape(2, 16)


def solution(mesh):
    return jax.shard_map(
        shards,
        mesh=mesh,
        in_specs=(
            P("slab", "energy"),
            P("slab", "energy"),
            P("slab", "energy"),
            P(),
            P("slab", "energy", None),
            P("slab", None),
            P("energy"),
            P("energy"),
            P(None, "energy", "slab", None),
        ),
        out_specs=P("slab", "energy"),
        check_vma=False,
    )
```
